256 devices in a mesh: gx: 4 (over y), gy: 8 (over z), gz: 8 (over x, core).
Axes of the slice: x: 4, y: 4, z: 8, core: 2. Of those that a mesh axis runs over, the one named last changes fastest.
Arguments:
- seg_state: float32 [4, 8, 8, 32, 9, 128], P('gx', 'gy', 'gz'), as said below
- seg_cells: int32 [4, 8, 8, 32, 128], P('gx', 'gy', 'gz'), may hold values from 0 to 15
- seg_nodes: int32 [4, 8, 8, 2, 4096], P('gx', 'gy', 'gz'), may hold values from 0 to 4095, each once within a row
- pair_blocks: int32 [4, 8, 8, 2, 128], P('gx', 'gy', 'gz'), may hold values from 0 to 31
- pair_offsets: int32 [4, 8, 8, 128], P('gx', 'gy', 'gz'), may hold values from 0 to 26
- pair_count: int32 [4, 8, 8], P('gx', 'gy', 'gz'), may hold values from 64 to 128, as said below
Outputs:
- node_velocity: float32 [4, 8, 8, 3, 4096], P('gx', 'gy', 'gz')
The draws below stay inside these ranges and needn't reach their ends.
Inputs may be any that keep to these rules, and one draw needn't show every extreme that they name: `seg_state`: rows 0 to 2 of the component dimension lie in [0, 1). `pair_count`: some domain has all 128 slots live, another exactly half of them.
All inputs are finite; a program needn't handle non-finite values.
Results may differ from the reference program's by a relative error of at most 0.0003.
Values sent between devices are 32-bit elements; how exact they have to be, the bound alone decides.
A program may use at most 64 MiB of HBM per device.

```python
import jax
import jax.numpy as jnp
from jax import lax

SEG_BLOCK = 128
BLK_DEV = 32
PAIR_SLOTS = 128
CELLS = 16
SEG_DEV = 4096
CELL_DEV = 16
N_GX = 4
N_GY = 8
N_GZ = 8


def draw_seg_state(key, part):
    key = jax.random.fold_in(key, 3)
    key_pos, key_dir = jax.random.split(key, 2)
    leading = (N_GX, N_GY, N_GZ, BLK_DEV)
    positions = jax.random.uniform(key_pos, leading + (3, SEG_BLOCK), jnp.float32)
    vectors = jax.random.normal(key_dir, leading + (6, SEG_BLOCK), jnp.float32)
    return jnp.concatenate([positions, vectors], axis=4)


def draw_pair_count(key, part):
    key = jax.random.fold_in(key, 7)
    key_counts, key_busy, key_quiet = jax.random.split(key, 3)
    domains = N_GX * N_GY * N_GZ
    counts = jax.random.randint(key_counts, (domains,), PAIR_SLOTS // 2, PAIR_SLOTS + 1)
    busiest = jax.random.randint(key_busy, (), 0, domains)
    quietest = (busiest + jax.random.randint(key_quiet, (), 1, domains)) % domains
    counts = counts.at[busiest].set(PAIR_SLOTS)
    counts = counts.at[quietest].set(PAIR_SLOTS // 2)
    return counts.reshape(N_GX, N_GY, N_GZ).astype(jnp.int32)


def place_ends(drawn, rng, low, top_value):
    dims = drawn.shape
    index_at = [jax.random.randint(jax.random.fold_in(rng, axis), (), 0, dims[axis]) for axis in range(len(dims))]
    drawn = drawn.at[tuple(index_at)].set(low)
    longest = dims.index(max(dims))
    index_at[longest] = (index_at[longest] + 1) % dims[longest]
    return drawn.at[tuple(index_at)].set(top_value)


def setup_inputs(seed: int = 0) -> dict:
    streams_of = jax.random.split(jax.random.key(seed), 7)
    seg_state = draw_seg_state(jax.random.fold_in(streams_of[6], 71), 0)
    seg_cells = place_ends(jax.random.randint(streams_of[1], (N_GX, N_GY, N_GZ, BLK_DEV, SEG_BLOCK), 0, CELL_DEV), jax.random.fold_in(streams_of[1], 1), 0, CELL_DEV - 1).astype(jnp.int32)
    seg_nodes = jax.vmap(lambda own: jax.random.permutation(own, SEG_DEV))(jax.random.split(streams_of[2], N_GX * N_GY * N_GZ * 2)).reshape((N_GX, N_GY, N_GZ, 2, SEG_DEV)).astype(jnp.int32)
    pair_blocks = place_ends(jax.random.randint(streams_of[3], (N_GX, N_GY, N_GZ, 2, PAIR_SLOTS), 0, BLK_DEV), jax.random.fold_in(streams_of[3], 1), 0, BLK_DEV - 1).astype(jnp.int32)
    pair_offsets = place_ends(jax.random.randint(streams_of[4], (N_GX, N_GY, N_GZ, PAIR_SLOTS), 0, 27), jax.random.fold_in(streams_of[4], 1), 0, 26).astype(jnp.int32)
    pair_count = draw_pair_count(jax.random.fold_in(streams_of[6], 71), 0)
    return dict(seg_state=seg_state, seg_cells=seg_cells, seg_nodes=seg_nodes, pair_blocks=pair_blocks, pair_offsets=pair_offsets, pair_count=pair_count)


PAIR_STRENGTH = 0.1
CORE_SQUARED = 0.2
FAR_STRENGTH = 0.008
DRAG_FLOOR = 0.5

def outer_dot(first_vec, second_vec):
    return first_vec[0][:, None] * second_vec[0][None, :] + first_vec[1][:, None] * second_vec[1][None, :] + first_vec[2][:, None] * second_vec[2][None, :]

def tile_force(own_tile, other_tile, shift):
    own_pos = own_tile[0:3]
    own_line = own_tile[3:6]
    own_burgers = own_tile[6:9]
    other_pos = other_tile[0:3] + shift[:, None]
    other_line = other_tile[3:6]
    other_burgers = other_tile[6:9]
    separation = own_pos[:, :, None] - other_pos[:, None, :]
    radius_sq = separation[0] * separation[0] + separation[1] * separation[1] + separation[2] * separation[2] + CORE_SQUARED
    inverse = lax.rsqrt(radius_sq)
    inv_cube = inverse * inverse * inverse
    inv_fifth = inv_cube * inverse * inverse
    coupling = outer_dot(own_burgers, other_burgers) * outer_dot(own_line, other_line)
    crossed = outer_dot(own_burgers, other_line) * outer_dot(own_line, other_burgers)
    strength = PAIR_STRENGTH * (coupling * inv_cube + CORE_SQUARED * crossed * inv_fifth)
    weighted = strength[None] * separation
    return (lax.optimization_barrier(jnp.sum(weighted, axis=2)), -lax.optimization_barrier(jnp.sum(weighted, axis=1)))

def cell_coords(flat_ids, grid_x, grid_y, grid_z):
    span_x = CELLS // grid_x
    span_y = CELLS // grid_y
    span_z = CELLS // grid_z
    per_domain = span_x * span_y * span_z
    owner = flat_ids // per_domain
    local_ids = flat_ids % per_domain
    owner_x = owner // (grid_y * grid_z)
    owner_y = owner // grid_z % grid_y
    owner_z = owner % grid_z
    inner_x = local_ids // (span_y * span_z)
    inner_y = local_ids // span_z % span_y
    inner_z = local_ids % span_z
    return (owner_x * span_x + inner_x, owner_y * span_y + inner_y, owner_z * span_z + inner_z)

def far_kernel(targets, grid_x, grid_y, grid_z):
    every_cell = jnp.arange(CELLS ** 3, dtype=jnp.int32)
    source = cell_coords(every_cell, grid_x, grid_y, grid_z)
    target = cell_coords(targets, grid_x, grid_y, grid_z)
    half = CELLS // 2
    deltas = [(source[k][:, None] - target[k][None, :] + half) % CELLS - half for k in range(3)]
    largest = jnp.maximum(jnp.maximum(jnp.abs(deltas[0]), jnp.abs(deltas[1])), jnp.abs(deltas[2]))
    dist_sq = (deltas[0] * deltas[0] + deltas[1] * deltas[1] + deltas[2] * deltas[2]).astype(jnp.float32)
    return jnp.where(largest > 1, FAR_STRENGTH * lax.rsqrt(jnp.maximum(dist_sq, 1.0)), jnp.float32(0.0))

def layout(blocks):
    return jnp.transpose(blocks, (1, 0, 2)).reshape(blocks.shape[1], -1)

def moment_terms(line, burgers, cell_hot):
    products = (burgers[:, None, :] * line[None, :, :]).reshape(9, -1)
    return jnp.dot(products, cell_hot, precision=lax.Precision.HIGHEST)

def segment_far(local_field, cell_hot, line, burgers):
    per_seg = jnp.dot(local_field, cell_hot.T, precision=lax.Precision.HIGHEST)
    pulled = [per_seg[3 * k] * burgers[0] + per_seg[3 * k + 1] * burgers[1] + per_seg[3 * k + 2] * burgers[2] for k in range(3)]
    return jnp.stack([pulled[1] * line[2] - pulled[2] * line[1], pulled[2] * line[0] - pulled[0] * line[2], pulled[0] * line[1] - pulled[1] * line[0]])

def node_velocity_of(seg_force, line, nodes):
    seg_total = seg_force.shape[1]
    length = jnp.sqrt(line[0] * line[0] + line[1] * line[1] + line[2] * line[2])
    halves = 0.5 * jnp.concatenate([seg_force, length[None]], axis=0)
    block_rows = 512 if seg_total % 512 == 0 else seg_total
    node_ids = jnp.arange(seg_total, dtype=jnp.int32)

    def add_block(turn_index, totals):
        first_slot = turn_index * block_rows
        part_rows = lax.dynamic_slice_in_dim(halves, first_slot, block_rows, 1)
        ends = lax.dynamic_slice_in_dim(nodes, first_slot, block_rows, 1)
        node_hot = (ends[0][:, None] == node_ids[None, :]).astype(jnp.float32) + (ends[1][:, None] == node_ids[None, :]).astype(jnp.float32)
        return totals + jnp.dot(part_rows, node_hot, precision=lax.Precision.HIGHEST)
    totals = lax.fori_loop(0, seg_total // block_rows, add_block, jnp.zeros((4, seg_total), jnp.float32))
    return totals[:3] / jnp.maximum(totals[3], DRAG_FLOOR)

def reference(seg_state, seg_cells, seg_nodes, pair_blocks, pair_offsets, pair_count):
    domains = N_GX * N_GY * N_GZ
    blocks = seg_state.shape[3]
    seg_total = blocks * seg_state.shape[5]

    def domain_pairs(domain, forces):
        home_x = domain // (N_GY * N_GZ)
        home_y = domain // N_GZ % N_GY
        home_z = domain % N_GZ
        live_count = pair_count[home_x, home_y, home_z]

        def one_pair(slot_index, forces):
            first_block = pair_blocks[home_x, home_y, home_z, 0, slot_index]
            second_block = pair_blocks[home_x, home_y, home_z, 1, slot_index]
            code_value = pair_offsets[home_x, home_y, home_z, slot_index]
            offset_x = code_value // 9 - 1
            offset_y = code_value // 3 % 3 - 1
            offset_z = code_value % 3 - 1
            peer_x = (home_x + offset_x) % N_GX
            peer_y = (home_y + offset_y) % N_GY
            peer_z = (home_z + offset_z) % N_GZ
            shift = jnp.stack([offset_x, offset_y, offset_z]).astype(jnp.float32)
            on_own, on_peer = tile_force(seg_state[home_x, home_y, home_z, first_block], seg_state[peer_x, peer_y, peer_z, second_block], shift)
            forces = forces.at[home_x, home_y, home_z, first_block].add(on_own)
            return forces.at[peer_x, peer_y, peer_z, second_block].add(on_peer)
        return lax.fori_loop(0, live_count, one_pair, forces)
    near_grid = lax.fori_loop(0, domains, domain_pairs, jnp.zeros((N_GX, N_GY, N_GZ, blocks, 3, seg_state.shape[5]), jnp.float32))
    flat_state = seg_state.reshape(domains, blocks, 9, seg_state.shape[5])
    flat_near = near_grid.reshape(domains, blocks, 3, seg_state.shape[5])
    cells_flat = seg_cells.reshape(domains, seg_total)
    nodes_flat = seg_nodes.reshape(domains, 2, seg_total)
    cell_ids = jnp.arange(CELL_DEV, dtype=jnp.int32)

    def moments_of(domain):
        columns = layout(flat_state[domain])
        cell_hot = (cells_flat[domain][:, None] == cell_ids[None, :]).astype(jnp.float32)
        return moment_terms(columns[3:6], columns[6:9], cell_hot)
    all_moments = lax.map(moments_of, jnp.arange(domains, dtype=jnp.int32))
    all_moments = jnp.transpose(all_moments, (1, 0, 2)).reshape(9, domains * CELL_DEV)

    def velocity_of(domain):
        columns = layout(flat_state[domain])
        cell_hot = (cells_flat[domain][:, None] == cell_ids[None, :]).astype(jnp.float32)
        targets = domain * CELL_DEV + cell_ids
        kernel = far_kernel(targets, N_GX, N_GY, N_GZ)
        local_field = jnp.dot(all_moments, kernel, precision=lax.Precision.HIGHEST)
        seg_force = layout(flat_near[domain]) + segment_far(local_field, cell_hot, columns[3:6], columns[6:9])
        return node_velocity_of(seg_force, columns[3:6], nodes_flat[domain])
    velocity = lax.map(velocity_of, jnp.arange(domains, dtype=jnp.int32))
    return velocity.reshape(N_GX, N_GY, N_GZ, 3, seg_total)
```

```python
import jax
import jax.numpy as jnp
import ml_dtypes
import numpy as np
from jax import lax
from jax.experimental import pallas as pl
from jax.experimental.pallas import tpu as pltpu
from jax.sharding import PartitionSpec as P

CELLS = 16
PAIR_STRENGTH = 0.1
CORE_SQUARED = 0.2
FAR_STRENGTH = 0.008
DRAG_FLOOR = 0.5

BLOCKS = 32
WIDTH = 128
SLOTS = 128
TILES = 36
CELL_DEV = 16
UNROLL = 4
SIDES = (-1, 0, 1)
F32 = jnp.float32
BF16 = jnp.bfloat16
MESH = pl.DeviceIdType.MESH
NT = (((1,), (1,)), ((), ()))
PAIR_SCALE = float(PAIR_STRENGTH * (1.0 / CORE_SQUARED) ** 1.5)
OWN, ON, OFF = 0, 1, 2


def ghost_slot(dx, dy, role):
    return role * 9 + (dx + 1) * 3 + dy + 1


def dot(first, second):
    return jnp.dot(first, second, preferred_element_type=F32)


def dot_nt(first, second):
    return lax.dot_general(first, second, NT, preferred_element_type=F32)


def head(value):
    return value.astype(BF16).astype(F32)


def pair16(low, high):
    return jnp.concatenate([low, high], axis=0).astype(BF16)


def row_ids(shape):
    return lax.broadcasted_iota(jnp.int32, shape, 0)


def block_rows(tile, last, rows):
    zero = jnp.zeros_like(tile)
    line = jnp.where(rows < 3, tile, zero)
    place = jnp.where((rows >= 3) & (rows < 6), tile, zero)
    burgers = jnp.where(rows == 2, last, pltpu.roll(tile, 2, 0))
    burgers = jnp.where(rows < 3, burgers, zero)
    return line, place, burgers


def prepare_block(i, dom, feats, weights_rows):
    rows = row_ids((8, WIDTH))
    tile = dom[i]
    tile = tile - jnp.where((rows >= 3) & (rows < 6), 0.5, 0.0)
    last = dom[32 + (i >> 3), pl.ds(i & 7, 1), :]
    line, place, burgers = block_rows(tile, last, rows)
    norm = jnp.sum(place * place, axis=0, keepdims=True)
    scale = 1.0 / CORE_SQUARED
    low = line - 2.0 * scale * place
    high = burgers + jnp.where(rows == 3, scale, jnp.where(rows == 4, scale * norm + 1.0, 0.0))
    full = jnp.concatenate([low, high], axis=0)
    first = head(full)
    second = head(full - first)
    third = head(full - first - second)
    stack = jnp.concatenate(
        [first, first, second, first, second, third, jnp.zeros((32, WIDTH), F32)], axis=0
    )
    feats[i] = jnp.transpose(stack).astype(BF16)
    place_first = head(place)
    ones = jnp.where(rows == 0, 1.0, 0.0)
    held = pair16(place_first + ones, place - place_first)
    weights_rows[i] = jnp.concatenate([held, held], axis=1)


def pair_group(group, meta, dom, ghosts, shifts, feats, weights_rows, own_out, peer_out, unroll):
    rows = row_ids((8, WIDTH))
    zero = jnp.zeros((8, WIDTH), F32)
    centre = jnp.where((rows >= 3) & (rows < 6), 0.5, 0.0)
    ones = jnp.where(rows == 0, 1.0, 0.0)
    loaded = []
    for u in range(unroll):
        slot = group * unroll + u
        i = meta[0, slot]
        g = meta[1, slot]
        j = meta[2, slot]
        tile = ghosts[g, j] + shifts[g]
        last = ghosts[g, 32 + (j >> 3), pl.ds(j & 7, 1), :]
        line, place, burgers = block_rows(tile, last, rows)
        norm = jnp.sum(place * place, axis=0, keepdims=True)
        extra = jnp.where(rows == 3, norm, jnp.where(rows == 4, 1.0, 0.0))
        line_1 = head(line)
        line_2 = line - line_1
        burgers_1 = head(burgers)
        burgers_2 = burgers - burgers_1
        place_1 = head(place)
        place_r = place - place_1
        place_2 = head(place_r)
        extra_1 = head(extra)
        extra_r = extra - extra_1
        extra_2 = head(extra_r)
        top = jnp.concatenate(
            [pair16(line_1, zero), pair16(zero, burgers_1), pair16(burgers_1, zero), pair16(zero, line_1)], axis=1
        )
        mid = jnp.concatenate(
            [pair16(line_2, zero), pair16(zero, burgers_2), pair16(burgers_2, zero), pair16(zero, line_2)], axis=1
        )
        products = jnp.concatenate([top, mid, top], axis=0)
        dist_1 = pair16(place_1, extra_1)
        dist_2 = pair16(place_2, extra_2)
        dist_3 = pair16(place_r - place_2, extra_r - extra_2)
        dists = jnp.concatenate([dist_1, dist_2, dist_1, dist_3, dist_2, dist_1], axis=0)
        held = pair16(place_1 + ones, place_r)
        held = jnp.concatenate([held, held], axis=1)
        loaded.append((slot, i, place, products, dists, held))
    outs = []
    for slot, i, place, products, dists, held in loaded:
        feat = feats[i]
        outs.append((dot(feat[:, :48], products), dot(feat[:, :96], dists)))
    strengths = []
    for four, dist in outs:
        inv = lax.rsqrt(dist)
        inv_sq = inv * inv
        line_line = four[:, 0:128]
        burgers_burgers = four[:, 128:256]
        line_burgers = four[:, 256:384]
        burgers_line = four[:, 384:512]
        strength = (inv_sq * inv) * (line_line * burgers_burgers + (line_burgers * burgers_line) * inv_sq)
        high = strength.astype(BF16)
        low = (strength - high.astype(F32)).astype(BF16)
        strengths.append((high, low))
    for (slot, i, place, products, dists, held), (high, low) in zip(loaded, strengths):
        peer = dot(weights_rows[i], jnp.concatenate([high, low], axis=0))
        own = dot_nt(held, jnp.concatenate([high, low], axis=1))
        peer = peer[0:8] + peer[8:16]
        own = own[0:8] + own[8:16]
        home = dom[i] - centre
        own_out[slot] = home * own[0:1] - own
        peer_out[slot] = place * peer[0:1] - peer


def slot_table(slot_out, live):
    keep = row_ids((SLOTS, WIDTH)) < live
    parts = [
        jnp.where(keep, PAIR_SCALE * slot_out[:, 3 + c, :], 0.0) for c in range(3)
    ]
    table = jnp.concatenate(parts, axis=1)
    first = table.astype(BF16)
    return jnp.concatenate([first, (table - first.astype(F32)).astype(BF16)], axis=0)


def slot_hot(targets, base, count):
    ids = row_ids((count, SLOTS)) + base
    hot = jnp.where(ids == targets, 1.0, 0.0).astype(BF16)
    return jnp.concatenate([hot, hot], axis=1)


def moment_block(b, dom, cells, total):
    rows = row_ids((8, WIDTH))
    tile = dom[b]
    last = dom[32 + (b >> 3), pl.ds(b & 7, 1), :]
    line, _, burgers = block_rows(tile, last, rows)
    hot = row_ids((CELL_DEV, WIDTH)) == cells[pl.ds(b, 1), :]
    line_1 = head(line)
    line_2 = line - line_1
    burgers_1 = head(burgers)
    burgers_2 = burgers - burgers_1
    zero = jnp.zeros((CELL_DEV, WIDTH), F32)
    spread = [
        jnp.concatenate([jnp.where(hot, part[k : k + 1], zero) for k in range(3)], axis=0).astype(BF16)
        for part in (line_1, line_2)
    ]
    pad = jnp.zeros((8, WIDTH), F32)
    left = jnp.concatenate([pair16(burgers_1, pad), pair16(burgers_1, pad), pair16(burgers_2, pad)], axis=1)
    right = jnp.concatenate([spread[0], spread[1], spread[0]], axis=1)
    return total + dot_nt(left, right)


def node_onehot(b, nodes, node_hot):
    lows = [
        jnp.where(row_ids((128, WIDTH)) == (nodes[e, pl.ds(b, 1), :] & 127), 1.0, 0.0).astype(BF16)
        for e in range(2)
    ]
    node_hot[b] = jnp.concatenate(lows, axis=1)


def node_block(b, nodes, node_hot, values, count, total):
    ends = []
    for e in range(2):
        high = nodes[e, pl.ds(b, 1), :] >> 7
        hit = row_ids((32, WIDTH)) == high
        parts = [jnp.where(hit, values[c, pl.ds(b, 1), :], 0.0) for c in range(2 * count)]
        ends.append(jnp.concatenate(parts, axis=0).astype(BF16))
    return total + dot_nt(jnp.concatenate(ends, axis=1), node_hot[b])


def far_tables():
    index = np.arange(CELL_DEV)
    inner = np.stack([index // 4, index // 2 % 2, index % 2])
    rel = np.arange(256)
    away = np.stack([rel // 64 * 4, rel // 8 % 8 * 2, rel % 8 * 2])
    delta = away[:, None, None, :] + inner[:, :, None, None] - inner[:, None, :, None]
    delta = (delta + 8) % 16 - 8
    dist = np.sqrt(np.maximum((delta.astype(np.float64) ** 2).sum(0), 1.0))
    far = np.where(np.abs(delta).max(0) > 1, FAR_STRENGTH / dist, 0.0).astype(np.float32)
    far = far.reshape(256, 256)
    first = far.astype(ml_dtypes.bfloat16)
    second = (far - first.astype(np.float32)).astype(ml_dtypes.bfloat16)
    table = np.concatenate([first, first, second], axis=1)
    lanes = np.arange(384)
    part = lanes % 128
    fold = np.zeros((16, 384), np.float32)
    for lane in lanes[part < 48]:
        fold[3 * (lane // 128) + part[lane] // 16, lane] = 1.0
    fold = np.concatenate([fold, fold], axis=1).astype(ml_dtypes.bfloat16)
    return table, fold


def kernel(
    meta, pairs, dom, cells, nodes, far_table, fold, out,
    ghosts, shifts, feats, weights_rows, own_out, peer_out, react, from_on, from_off, from_layer,
    node_hot, node_len, values, group_z, group_xy,
    halo_send, halo_recv, react_send, react_recv, gather_send, gather_recv,
):
    size_x, size_y, size_z = 4, 8, 8
    me_x = lax.axis_index("gx")
    me_y = lax.axis_index("gy")
    me_z = lax.axis_index("gz")
    toward = 1 - 2 * lax.rem(me_z, 2)

    def at_x(d):
        return lax.rem(me_x + d + size_x, size_x)

    def at_y(d):
        return lax.rem(me_y + d + size_y, size_y)

    def at_role(role):
        if role == OWN:
            return me_z
        step = toward if role == ON else -toward
        return lax.rem(me_z + step + size_z, size_z)

    def device(dx, dy, role):
        return (at_x(dx), at_y(dy), at_role(role))

    peers = [
        device(dx, dy, role)
        for role in (OWN, ON, OFF)
        for dx in SIDES
        for dy in SIDES
        if (dx, dy, role) != (0, 0, OWN)
    ]
    peers += [(at_x(2), me_y, me_z)]
    peers += [(me_x, at_y(r), me_z) for r in range(2, size_y - 1)]
    peers += [(me_x, me_y, lax.rem(me_z + r, size_z)) for r in range(2, size_z - 1)]

    barrier = pltpu.get_barrier_semaphore()
    for peer in peers:
        pl.semaphore_signal(barrier, inc=1, device_id=peer, device_id_type=MESH)
    pl.semaphore_wait(barrier, len(peers))

    halo = []

    def send_ghost(source, target, slot):
        copy = pltpu.make_async_remote_copy(
            src_ref=source,
            dst_ref=ghosts.at[slot],
            send_sem=halo_send.at[len(halo)],
            recv_sem=halo_recv.at[slot],
            device_id=target,
            device_id_type=MESH,
        )
        copy.start()
        halo.append(copy)

    def await_ghost(slot):
        pltpu.make_async_remote_copy(
            src_ref=dom,
            dst_ref=ghosts.at[slot],
            send_sem=halo_send.at[0],
            recv_sem=halo_recv.at[slot],
            device_id=device(0, 0, ON),
            device_id_type=MESH,
        ).wait_recv()

    for e in (-1, 1):
        send_ghost(dom, device(0, e, OWN), ghost_slot(0, -e, OWN))
    for e in (-1, 1):
        send_ghost(dom, device(e, 0, OWN), ghost_slot(-e, 0, OWN))
    send_ghost(dom, device(0, 0, OFF), ghost_slot(0, 0, OFF))
    send_ghost(dom, device(0, 0, ON), ghost_slot(0, 0, ON))

    ghosts[ghost_slot(0, 0, OWN)] = dom[...]
    rows = row_ids((8, WIDTH))
    for role in (OWN, ON, OFF):
        away_z = 0 if role == OWN else (toward if role == ON else -toward)
        away_z = jnp.asarray(away_z, jnp.int32).astype(F32) - 0.5
        for dx in SIDES:
            for dy in SIDES:
                shifts[ghost_slot(dx, dy, role)] = jnp.where(
                    rows == 3,
                    dx - 0.5,
                    jnp.where(rows == 4, dy - 0.5, jnp.where(rows == 5, away_z, 0.0)),
                )

    def features(b, carry):
        prepare_block(b, dom, feats, weights_rows)
        return carry

    lax.fori_loop(0, 16, features, 0)

    for dx in (-1, 1):
        slot = ghost_slot(dx, 0, OWN)
        await_ghost(slot)
        send_ghost(ghosts.at[slot], device(0, 0, OFF), ghost_slot(dx, 0, OFF))
        send_ghost(ghosts.at[slot], device(0, 0, ON), ghost_slot(dx, 0, ON))
    for dy in (-1, 1):
        slot = ghost_slot(0, dy, OWN)
        await_ghost(slot)
        for e in (-1, 1):
            send_ghost(ghosts.at[slot], device(e, 0, OWN), ghost_slot(-e, dy, OWN))
        send_ghost(ghosts.at[slot], device(0, 0, OFF), ghost_slot(0, dy, OFF))
        send_ghost(ghosts.at[slot], device(0, 0, ON), ghost_slot(0, dy, ON))

    lax.fori_loop(16, BLOCKS, features, 0)

    for dx in (-1, 1):
        slot = ghost_slot(dx, 0, OFF)
        await_ghost(slot)
        for e in (-1, 1):
            send_ghost(ghosts.at[slot], device(0, e, OWN), ghost_slot(dx, -e, OFF))

    moments = lax.fori_loop(
        0, BLOCKS, lambda b, total: moment_block(b, dom, cells, total), jnp.zeros((16, 48), F32), unroll=2
    )
    group_z[0:8, :] = jnp.concatenate([moments[0:8], jnp.zeros((8, 80), F32)], axis=1)

    for dx in (-1, 1):
        for dy in (-1, 1):
            slot = ghost_slot(dx, dy, OWN)
            await_ghost(slot)
            send_ghost(ghosts.at[slot], device(0, 0, ON), ghost_slot(dx, dy, ON))

    def nodes_of(b, carry):
        node_onehot(b, nodes, node_hot)
        return carry

    lax.fori_loop(0, BLOCKS, nodes_of, 0)
    lines = [dom[0:BLOCKS, k, :] for k in range(3)]
    length = 0.5 * jnp.sqrt(lines[0] * lines[0] + lines[1] * lines[1] + lines[2] * lines[2])
    values[0] = head(length)
    values[1] = length - head(length)
    sums = lax.fori_loop(
        0,
        BLOCKS,
        lambda b, total: node_block(b, nodes, node_hot, values, 1, total),
        jnp.zeros((64, WIDTH), F32),
    )
    node_len[...] = jnp.maximum(sums[0:32] + sums[32:64], DRAG_FLOOR)

    for dx in SIDES:
        for dy in SIDES:
            await_ghost(ghost_slot(dx, dy, ON))
    await_ghost(ghost_slot(0, 0, OFF))
    for dy in (-1, 1):
        await_ghost(ghost_slot(0, dy, OFF))
    for dx in (-1, 1):
        for dy in (-1, 1):
            await_ghost(ghost_slot(dx, dy, OFF))

    gathers = []

    def gather(source, target_ref, target, number):
        copy = pltpu.make_async_remote_copy(
            src_ref=source,
            dst_ref=target_ref,
            send_sem=gather_send.at[number],
            recv_sem=gather_recv.at[number],
            device_id=target,
            device_id_type=MESH,
        )
        copy.start()
        gathers.append(copy)

    def pair_part(first, last):
        def body(group, carry):
            pair_group(
                group, meta, dom, ghosts, shifts, feats, weights_rows, own_out, peer_out, UNROLL
            )
            return carry

        lax.fori_loop(first // UNROLL, last // UNROLL, body, 0)

    for r in range(1, size_z):
        gather(
            group_z.at[pl.ds(0, 8)],
            group_z.at[pl.ds(8 * r, 8)],
            (me_x, me_y, lax.rem(me_z - r + size_z, size_z)),
            r - 1,
        )
    pair_part(0, 48)
    for copy in gathers[0:7]:
        copy.wait_recv()
    for a in range(3):
        group_xy[0, 0, 8 * a : 8 * a + 8, :] = group_z[pl.ds(a, 8, stride=8), :]
    for r in range(1, size_y):
        gather(group_xy.at[0, 0], group_xy.at[0, r], (me_x, at_y(-r), me_z), 6 + r)
    pair_part(48, 88)
    for copy in gathers[7:14]:
        copy.wait_recv()
    for r in range(1, size_x):
        gather(group_xy.at[0], group_xy.at[r], (at_x(-r), me_y, me_z), 13 + r)
    pair_part(88, SLOTS)

    live = meta[4, 0]
    table = slot_table(peer_out, live)
    targets = pairs[3:4, :]
    reacts = []

    def send_react(source, target_ref, target, number):
        copy = pltpu.make_async_remote_copy(
            src_ref=source,
            dst_ref=target_ref,
            send_sem=react_send.at[number],
            recv_sem=react_recv.at[number],
            device_id=target,
            device_id_type=MESH,
        )
        copy.start()
        reacts.append(copy)

    react[ON] = dot(slot_hot(targets, 288, 288), table)
    send_react(react.at[ON], from_on, device(0, 0, ON), 0)
    react[OFF] = dot(slot_hot(targets, 576, 288), table)
    for dx in SIDES:
        for dy in SIDES:
            d = ghost_slot(dx, dy, 0)
            send_react(
                react.at[OFF, pl.ds(32 * d, 32)], from_off.at[pl.ds(32 * d, 32)], device(dx, dy, OFF), 1 + d
            )
    react[OWN] = dot(slot_hot(targets, 0, 288), table)
    reacts[0].wait_recv()
    react[OWN] = react[OWN] + from_on[...]
    sent = [(dx, dy) for dx in SIDES for dy in SIDES if (dx, dy) != (0, 0)]
    for number, (dx, dy) in enumerate(sent):
        d = ghost_slot(dx, dy, 0)
        send_react(
            react.at[OWN, pl.ds(32 * d, 32)], from_layer.at[number], device(dx, dy, OWN), 10 + number
        )

    near = dot(slot_hot(pairs[0:1, :], 0, BLOCKS), slot_table(own_out, live))
    near = near + react[OWN, pl.ds(128, 32), :]

    for copy in gathers[14:17]:
        copy.wait_recv()
    sides = []
    for a in range(3):
        held = group_xy[:, :, 8 * a : 8 * a + 8, :].reshape(256, WIDTH)
        first = held.astype(BF16)
        second = (held - first.astype(F32)).astype(BF16)
        sides.append(jnp.concatenate([first, second, first], axis=0))
    blocks = dot(far_table[...], jnp.concatenate(sides, axis=1))
    source = lax.broadcasted_iota(jnp.int32, (256, 384), 0) >> 4
    lane = lax.broadcasted_iota(jnp.int32, (256, 384), 1) & 15
    blocks = jnp.where(source == lane, blocks, 0.0)
    folded = blocks[0:16]
    for k in range(1, 16):
        folded = folded + blocks[16 * k : 16 * k + 16]
    folded = jnp.concatenate([folded, jnp.zeros((112, 384), F32)], axis=0)
    first = folded.astype(BF16)
    second = (folded - first.astype(F32)).astype(BF16)
    field = dot_nt(fold[...], jnp.concatenate([first, second], axis=1))
    cell = cells[...]
    hits = [cell == m for m in range(CELL_DEV)]
    per_seg = []
    for m in range(9):
        held = jnp.zeros((BLOCKS, WIDTH), F32)
        for k in range(CELL_DEV):
            held = jnp.where(hits[k], field[m : m + 1, k : k + 1], held)
        per_seg.append(held)
    burgers = [dom[0:BLOCKS, 6, :], dom[0:BLOCKS, 7, :], dom[BLOCKS:TILES].reshape(BLOCKS, WIDTH)]
    lines = [dom[0:BLOCKS, k, :] for k in range(3)]
    pulled = [sum(per_seg[3 * a + k] * burgers[k] for k in range(3)) for a in range(3)]
    force = [
        pulled[1] * lines[2] - pulled[2] * lines[1],
        pulled[2] * lines[0] - pulled[0] * lines[2],
        pulled[0] * lines[1] - pulled[1] * lines[0],
    ]

    for copy in reacts[1:]:
        copy.wait_recv()
    for number in range(8):
        near = near + from_layer[number]
    for d in range(9):
        near = near + from_off[pl.ds(32 * d, 32), :]
    for c in range(3):
        half = 0.5 * (force[c] + near[:, 128 * c : 128 * c + 128])
        values[c] = head(half)
        values[3 + c] = half - head(half)
    sums = lax.fori_loop(
        0,
        BLOCKS,
        lambda b, total: node_block(b, nodes, node_hot, values, 3, total),
        jnp.zeros((192, WIDTH), F32),
        unroll=2,
    )
    for c in range(3):
        out[c] = (sums[32 * c : 32 * c + 32] + sums[96 + 32 * c : 128 + 32 * c]) / node_len[...]

    for copy in halo + gathers + reacts:
        copy.wait_send()


def shards(seg_state, seg_cells, seg_nodes, pair_blocks, pair_offsets, pair_count):
    own = seg_state[0, 0, 0]
    tiles = jnp.concatenate([own[:, 3:6], own[:, 0:3], own[:, 6:8]], axis=1)
    dom = jnp.concatenate([tiles, own[:, 8].reshape(4, 8, WIDTH)], axis=0)
    cells = seg_cells[0, 0, 0]
    nodes = seg_nodes[0, 0, 0].reshape(2, BLOCKS, WIDTH)
    first, second = pair_blocks[0, 0, 0, 0], pair_blocks[0, 0, 0, 1]
    codes = pair_offsets[0, 0, 0]
    toward = 1 - 2 * (lax.axis_index("gz") % 2)
    away_z = codes % 3 - 1
    role = jnp.where(away_z == 0, OWN, jnp.where(away_z == toward, ON, OFF))
    domain = role * 9 + codes // 3
    live = jnp.broadcast_to(pair_count[0, 0, 0], (SLOTS,))
    empty = jnp.zeros_like(codes)
    meta = jnp.stack([first, domain, second, domain * BLOCKS + second, live, empty, empty, empty])
    far_table, fold = far_tables()
    vmem = pl.BlockSpec(memory_space=pltpu.VMEM)
    out = pl.pallas_call(
        kernel,
        out_shape=jax.ShapeDtypeStruct((3, BLOCKS, WIDTH), F32),
        in_specs=[pl.BlockSpec(memory_space=pltpu.SMEM)] + [vmem] * 6,
        out_specs=vmem,
        scratch_shapes=[
            pltpu.VMEM((27, TILES, 8, WIDTH), F32),
            pltpu.VMEM((27, 8, WIDTH), F32),
            pltpu.VMEM((BLOCKS, 128, WIDTH), BF16),
            pltpu.VMEM((BLOCKS, 16, 256), BF16),
            pltpu.VMEM((SLOTS, 8, WIDTH), F32),
            pltpu.VMEM((SLOTS, 8, WIDTH), F32),
            pltpu.VMEM((3, 288, 384), F32),
            pltpu.VMEM((288, 384), F32),
            pltpu.VMEM((288, 384), F32),
            pltpu.VMEM((8, 32, 384), F32),
            pltpu.VMEM((BLOCKS, 128, 256), BF16),
            pltpu.VMEM((32, WIDTH), F32),
            pltpu.VMEM((6, BLOCKS, WIDTH), F32),
            pltpu.VMEM((64, WIDTH), F32),
            pltpu.VMEM((4, 8, 24, WIDTH), F32),
            pltpu.SemaphoreType.DMA((26,)),
            pltpu.SemaphoreType.DMA((27,)),
            pltpu.SemaphoreType.DMA((18,)),
            pltpu.SemaphoreType.DMA((18,)),
            pltpu.SemaphoreType.DMA((17,)),
            pltpu.SemaphoreType.DMA((17,)),
        ],
        compiler_params=pltpu.CompilerParams(
            collective_id=0, has_side_effects=True, vmem_limit_bytes=40 * 1024 * 1024
        ),
    )(meta, meta, dom, cells, nodes, jnp.asarray(far_table), jnp.asarray(fold))
    return out.reshape(1, 1, 1, 3, BLOCKS * WIDTH)


def solution(mesh):
    placed = (
        P("gx", "gy", "gz", None, None, None),
        P("gx", "gy", "gz", None, None),
        P("gx", "gy", "gz", None, None),
        P("gx", "gy", "gz", None, None),
        P("gx", "gy", "gz", None),
        P("gx", "gy", "gz"),
    )
    return jax.shard_map(
        shards,
        mesh=mesh,
        in_specs=placed,
        out_specs=P("gx", "gy", "gz", None, None),
        check_vma=False,
    )
```

```python
import jax
import jax.numpy as jnp
import ml_dtypes
import numpy as np
from jax import lax
from jax.experimental import pallas as pl
from jax.experimental.pallas import tpu as pltpu
from jax.sharding import PartitionSpec as P

CELLS = 16
PAIR_STRENGTH = 0.1
CORE_SQUARED = 0.2
FAR_STRENGTH = 0.008
DRAG_FLOOR = 0.5

BLOCKS = 32
WIDTH = 128
SLOTS = 128
TILES = 36
CELL_DEV = 16
UNROLL = 8
SIDES = (-1, 0, 1)
F32 = jnp.float32
BF16 = jnp.bfloat16
MESH = pl.DeviceIdType.MESH
NT = (((1,), (1,)), ((), ()))
PAIR_SCALE = float(PAIR_STRENGTH * (1.0 / CORE_SQUARED) ** 1.5)
OWN, ON, OFF = 0, 1, 2


def ghost_slot(dx, dy, role):
    return role * 9 + (dx + 1) * 3 + dy + 1


def dot(first, second):
    return jnp.dot(first, second, preferred_element_type=F32)


def dot_nt(first, second):
    return lax.dot_general(first, second, NT, preferred_element_type=F32)


def head(value):
    return value.astype(BF16).astype(F32)


def pair16(low, high):
    return jnp.concatenate([low, high], axis=0).astype(BF16)


def row_ids(shape):
    return lax.broadcasted_iota(jnp.int32, shape, 0)


def block_rows(tile, last, rows):
    zero = jnp.zeros_like(tile)
    middle = (rows >= 3) & (rows < 6)
    line = jnp.where(middle, tile, zero)
    place = jnp.where(rows < 3, tile, zero)
    burgers = jnp.where(rows == 5, last, pltpu.roll(tile, 5, 0))
    burgers = jnp.where(middle, burgers, zero)
    return line, place, burgers


def prepare_block(i, dom, feats, weights_rows):
    rows = row_ids((8, WIDTH))
    tile = dom[i]
    tile = tile - jnp.where(rows < 3, 0.5, 0.0)
    last = dom[32 + (i >> 3), pl.ds(i & 7, 1), :]
    line, place, burgers = block_rows(tile, last, rows)
    norm = jnp.sum(place * place, axis=0, keepdims=True)
    scale = 1.0 / CORE_SQUARED
    low = line - 2.0 * scale * place
    high = burgers + jnp.where(rows == 0, scale, jnp.where(rows == 1, scale * norm + 1.0, 0.0))
    full = jnp.concatenate([low, high], axis=0)
    first = head(full)
    second = head(full - first)
    third = head(full - first - second)
    stack = jnp.concatenate(
        [first, first, second, first, second, third, jnp.zeros((32, WIDTH), F32)], axis=0
    )
    feats[i] = jnp.transpose(stack).astype(BF16)
    place_first = head(place)
    ones = jnp.where(rows == 3, 1.0, 0.0)
    held = pair16(place_first + ones, place - place_first)
    weights_rows[i] = jnp.concatenate([held, held], axis=1)


def pair_group(group, blocks, codes, dom, ghosts, shifts, feats, weights_rows, own_out, peer_out, unroll):
    rows = row_ids((8, WIDTH))
    zero = jnp.zeros((8, WIDTH), F32)
    centre = jnp.where(rows < 3, 0.5, 0.0)
    ones = jnp.where(rows == 3, 1.0, 0.0)
    loaded = []
    for u in range(unroll):
        slot = group * unroll + u
        i = blocks[0, slot]
        g = codes[0, slot]
        j = blocks[1, slot]
        tile = ghosts[g, j] + shifts[g]
        last = ghosts[g, 32 + (j >> 3), pl.ds(j & 7, 1), :]
        line, place, burgers = block_rows(tile, last, rows)
        norm = jnp.sum(place * place, axis=0, keepdims=True)
        extra = jnp.where(rows == 0, norm, jnp.where(rows == 1, 1.0, 0.0))
        line_1 = head(line)
        line_2 = line - line_1
        burgers_1 = head(burgers)
        burgers_2 = burgers - burgers_1
        place_1 = head(place)
        place_r = place - place_1
        place_2 = head(place_r)
        extra_1 = head(extra)
        extra_r = extra - extra_1
        extra_2 = head(extra_r)
        top = jnp.concatenate(
            [pair16(line_1, zero), pair16(zero, burgers_1), pair16(burgers_1, zero), pair16(zero, line_1)], axis=1
        )
        mid = jnp.concatenate(
            [pair16(line_2, zero), pair16(zero, burgers_2), pair16(burgers_2, zero), pair16(zero, line_2)], axis=1
        )
        products = jnp.concatenate([top, mid, top], axis=0)
        dist_1 = pair16(place_1, extra_1)
        dist_2 = pair16(place_2, extra_2)
        dist_3 = pair16(place_r - place_2, extra_r - extra_2)
        dists = jnp.concatenate([dist_1, dist_2, dist_1, dist_3, dist_2, dist_1], axis=0)
        held = pair16(place_1 + ones, place_r)
        held = jnp.concatenate([held, held], axis=1)
        loaded.append((slot, i, place, products, dists, held))
    outs = []
    for slot, i, place, products, dists, held in loaded:
        feat = feats[i]
        outs.append((dot(feat[:, :48], products), dot(feat[:, :96], dists)))
    strengths = []
    for four, dist in outs:
        inv = lax.rsqrt(dist)
        inv_sq = inv * inv
        line_line = four[:, 0:128]
        burgers_burgers = four[:, 128:256]
        line_burgers = four[:, 256:384]
        burgers_line = four[:, 384:512]
        strength = (inv_sq * inv) * (line_line * burgers_burgers + (line_burgers * burgers_line) * inv_sq)
        high = strength.astype(BF16)
        low = (strength - high.astype(F32)).astype(BF16)
        strengths.append((high, low))
    for (slot, i, place, products, dists, held), (high, low) in zip(loaded, strengths):
        peer = dot(weights_rows[i], jnp.concatenate([high, low], axis=0))
        own = dot_nt(held, jnp.concatenate([high, low], axis=1))
        peer = peer[0:8] + peer[8:16]
        own = own[0:8] + own[8:16]
        home = dom[i] - centre
        own_out[slot] = home * own[3:4] - own
        peer_out[slot] = place * peer[3:4] - peer


def slot_table(slot_out, live):
    keep = row_ids((SLOTS, WIDTH)) < live
    parts = [
        jnp.where(keep, PAIR_SCALE * slot_out[:, c, :], 0.0) for c in range(3)
    ]
    table = jnp.concatenate(parts, axis=1)
    first = table.astype(BF16)
    return jnp.concatenate([first, (table - first.astype(F32)).astype(BF16)], axis=0)


def slot_hot(targets, base, count):
    ids = row_ids((count, SLOTS)) + base
    hot = jnp.where(ids == targets, 1.0, 0.0).astype(BF16)
    return jnp.concatenate([hot, hot], axis=1)


def moment_block(b, dom, cells, total):
    rows = row_ids((8, WIDTH))
    tile = dom[b]
    last = dom[32 + (b >> 3), pl.ds(b & 7, 1), :]
    line, _, burgers = block_rows(tile, last, rows)
    hot = row_ids((CELL_DEV, WIDTH)) == cells[pl.ds(b, 1), :]
    line_1 = head(line)
    line_2 = line - line_1
    burgers_1 = head(burgers)
    burgers_2 = burgers - burgers_1
    zero = jnp.zeros((CELL_DEV, WIDTH), F32)
    spread = [
        jnp.concatenate([jnp.where(hot, part[3 + k : 4 + k], zero) for k in range(3)], axis=0).astype(BF16)
        for part in (line_1, line_2)
    ]
    pad = jnp.zeros((8, WIDTH), F32)
    left = jnp.concatenate([pair16(burgers_1, pad), pair16(burgers_1, pad), pair16(burgers_2, pad)], axis=1)
    right = jnp.concatenate([spread[0], spread[1], spread[0]], axis=1)
    return total + dot_nt(left, right)


def nodes_row(nodes, e, b):
    return nodes[e : e + 1, pl.ds(pl.multiple_of(b * WIDTH, WIDTH), WIDTH)]


def node_onehot(b, nodes, node_hot):
    lows = [
        jnp.where(row_ids((128, WIDTH)) == (nodes_row(nodes, e, b) & 127), 1.0, 0.0).astype(BF16)
        for e in range(2)
    ]
    node_hot[b] = jnp.concatenate(lows, axis=1)


def node_sums(nodes, node_hot, values, count):
    together = 4

    def body(turn, total):
        parts, hots = [], []
        for u in range(together):
            b = turn * together + u
            for e in range(2):
                hit = row_ids((32, WIDTH)) == nodes_row(nodes, e, b) >> 7
                rows = [jnp.where(hit, values[c, pl.ds(b, 1), :], 0.0) for c in range(2 * count)]
                parts.append(jnp.concatenate(rows, axis=0).astype(BF16))
            hots.append(node_hot[b])
        return total + dot_nt(jnp.concatenate(parts, axis=1), jnp.concatenate(hots, axis=1))

    return lax.fori_loop(0, BLOCKS // together, body, jnp.zeros((64 * count, WIDTH), F32))


def far_tables():
    index = np.arange(CELL_DEV)
    inner = np.stack([index // 4, index // 2 % 2, index % 2])
    rel = np.arange(256)
    away = np.stack([rel // 64 * 4, (rel // 8 % 8 - 3) * 2, (rel % 8 - 3) * 2])
    delta = away[:, None, None, :] + inner[:, :, None, None] - inner[:, None, :, None]
    delta = (delta + 8) % 16 - 8
    dist = np.sqrt(np.maximum((delta.astype(np.float64) ** 2).sum(0), 1.0))
    far = np.where(np.abs(delta).max(0) > 1, FAR_STRENGTH / dist, 0.0).astype(np.float32)
    far = far.reshape(256, 256)
    first = far.astype(ml_dtypes.bfloat16)
    second = (far - first.astype(np.float32)).astype(ml_dtypes.bfloat16)
    table = np.concatenate([first, first, second], axis=1)
    lanes = np.arange(384)
    part = lanes % 128
    fold = np.zeros((16, 384), np.float32)
    for lane in lanes[part < 48]:
        fold[3 * (lane // 128) + part[lane] // 16, lane] = 1.0
    fold = np.concatenate([fold, fold], axis=1).astype(ml_dtypes.bfloat16)
    return table, fold


def kernel(
    state_in, cells_in, nodes_in, blocks_in, codes_in, count, far_in, fold_in, out,
    raw, cells, nodes, block_ids, code_ids, blocks, codes, far_table, fold,
    dom, ghosts, shifts, feats, weights_rows, own_out, peer_out, react, from_on, from_off, from_layer,
    node_hot, node_len, values, group_z, group_xy,
    load_sem, halo_send, halo_recv, react_send, react_recv, gather_send, gather_recv,
):
    size_x, size_y, size_z = 4, 8, 8
    me_x = lax.axis_index("gx")
    me_y = lax.axis_index("gy")
    me_z = lax.axis_index("gz")
    toward = 1 - 2 * lax.rem(me_z, 2)

    loads = [
        pltpu.make_async_copy(source, target, load_sem.at[number])
        for number, (source, target) in enumerate(
            [
                (state_in, raw), (cells_in, cells), (nodes_in, nodes), (blocks_in, blocks), (codes_in, codes),
                (blocks_in, block_ids), (codes_in, code_ids), (far_in, far_table), (fold_in, fold),
            ]
        )
    ]
    for load in loads:
        load.start()

    def at_x(d):
        return lax.rem(me_x + d + size_x, size_x)

    def at_y(d):
        return lax.rem(me_y + d + size_y, size_y)

    def at_z(d):
        return lax.rem(me_z + d + size_z, size_z)

    def away(role):
        return 0 if role == OWN else (toward if role == ON else -toward)

    def device(dx, dy, role):
        return (at_x(dx), at_y(dy), at_z(away(role)))

    def code(dx, dy, dz):
        return (dx + 1) * 9 + (dy + 1) * 3 + dz + 1

    peers = [
        device(-1, 0, OWN), device(1, 0, OWN), device(0, -1, OWN), device(0, 1, OWN), device(0, 0, OFF), device(0, 0, ON)
    ]
    barrier = pltpu.get_barrier_semaphore()
    for peer in peers:
        pl.semaphore_signal(barrier, inc=1, device_id=peer, device_id_type=MESH)
    loads[0].wait()
    for k in range(8):
        dom[0:BLOCKS, k, :] = raw[k]
    dom[BLOCKS:TILES] = raw[8].reshape(4, 8, WIDTH)
    pl.semaphore_wait(barrier, len(peers))

    halo = []
    half = TILES // 2

    def piece(ref, part):
        return ref if part is None else ref.at[pl.ds(part * half, half)]

    def ghost(dx, dy, role):
        return ghosts.at[code(dx, dy, away(role))]

    def send_ghost(source, to, slot, offset, part):
        copy = pltpu.make_async_remote_copy(
            src_ref=piece(source, part),
            dst_ref=piece(ghosts.at[code(*offset)], part),
            send_sem=halo_send.at[len(halo)],
            recv_sem=halo_recv.at[2 * slot + (part or 0)],
            device_id=device(*to),
            device_id_type=MESH,
        )
        copy.start()
        halo.append(copy)

    def await_ghost(dx, dy, role, part=None):
        pltpu.make_async_remote_copy(
            src_ref=piece(dom, part),
            dst_ref=piece(ghost(dx, dy, role), part),
            send_sem=halo_send.at[0],
            recv_sem=halo_recv.at[2 * ghost_slot(dx, dy, role) + (part or 0)],
            device_id=device(0, 0, ON),
            device_id_type=MESH,
        ).wait_recv()

    def pass_x(source, e, dy, role, part):
        send_ghost(source, (e, 0, OWN), ghost_slot(-e, dy, role), (-e, dy, away(role)), part)

    def pass_y(source, e, dx, role, part):
        send_ghost(source, (0, e, OWN), ghost_slot(dx, -e, role), (dx, -e, away(role)), part)

    def pass_off(source, dx, dy, part):
        send_ghost(source, (0, 0, OFF), ghost_slot(dx, dy, OFF), (dx, dy, toward), part)

    def pass_on(source, dx, dy):
        send_ghost(source, (0, 0, ON), ghost_slot(dx, dy, ON), (dx, dy, -toward), None)

    for part in (0, 1):
        for e in (-1, 1):
            pass_y(dom, e, 0, OWN, part)
        for e in (-1, 1):
            pass_x(dom, e, 0, OWN, part)
        pass_off(dom, 0, 0, part)
    pass_on(dom, 0, 0)

    gathers = []

    def gather(source, target, to):
        number = len(gathers)
        copy = pltpu.make_async_remote_copy(
            src_ref=source,
            dst_ref=target,
            send_sem=gather_send.at[number],
            recv_sem=gather_recv.at[number],
            device_id=to,
            device_id_type=MESH,
        )
        copy.start()
        gathers.append(copy)
        return copy

    def spread_of_8(ref_of, at):
        for distance, moves in (
            (1, ((3, 4, 1, -1), (3, 2, 1, 1))),
            (2, ((3, 5, 2, -1), (2, 0, 2, 1))),
            (2, ((5, 7, 1, -1),)),
        ):
            sent = [
                gather(ref_of(first, count), ref_of(target, count), at(sign * distance))
                for first, target, count, sign in moves
            ]
            yield
            for copy in sent:
                copy.wait_recv()

    def gather_steps():
        yield from spread_of_8(
            lambda first, count: group_z.at[pl.ds(8 * first, 8 * count)], lambda d: (me_x, me_y, at_z(d))
        )
        for a in range(3):
            group_xy[0, 3, 8 * a : 8 * a + 8, :] = group_z[pl.ds(3 + a, 8, stride=8), :]
        yield from spread_of_8(
            lambda first, count: group_xy.at[0, pl.ds(first, count)], lambda d: (me_x, at_y(d), me_z)
        )
        sent = [
            gather(group_xy.at[0], group_xy.at[r], (at_x(-r), me_y, me_z)) for r in range(1, size_x)
        ]
        yield
        for copy in sent:
            copy.wait_recv()

    steps = gather_steps()

    def gather_step():
        next(steps, None)

    def features(b, carry):
        prepare_block(b, dom, feats, weights_rows)
        return carry

    def features_part(number):
        lax.fori_loop(4 * number, 4 * number + 4, features, 0, unroll=2)

    def nodes_of(b, carry):
        node_onehot(b, nodes, node_hot)
        return carry

    loads[1].wait()
    moments = lax.fori_loop(
        0, BLOCKS, lambda b, total: moment_block(b, dom, cells, total), jnp.zeros((16, 48), F32), unroll=4
    )
    group_z[24:32, :] = jnp.concatenate([moments[0:8], jnp.zeros((8, 80), F32)], axis=1)
    gather_step()

    for part in (0, 1):
        await_ghost(0, 0, OFF, part)
        for e in (-1, 1):
            pass_x(ghost(0, 0, OFF), e, 0, OFF, part)
    features_part(0)
    for part in (0, 1):
        for dx in (-1, 1):
            await_ghost(dx, 0, OWN, part)
            pass_y(ghost(dx, 0, OWN), -dx, dx, OWN, part)
    for dx in (-1, 1):
        pass_on(ghost(dx, 0, OWN), dx, 0)
    gather_step()
    features_part(1)
    for part in (0, 1):
        for dy in (-1, 1):
            await_ghost(0, dy, OWN, part)
            pass_x(ghost(0, dy, OWN), dy, dy, OWN, part)
            pass_off(ghost(0, dy, OWN), 0, dy, part)
    for dy in (-1, 1):
        pass_on(ghost(0, dy, OWN), 0, dy)
    gather_step()
    features_part(2)
    for part in (0, 1):
        for dx in (-1, 1):
            await_ghost(dx, 0, OFF, part)
            pass_y(ghost(dx, 0, OFF), dx, dx, OFF, part)
    features_part(3)
    gather_step()
    for part in (0, 1):
        for d in (-1, 1):
            await_ghost(d, d, OWN, part)
            pass_off(ghost(d, d, OWN), d, d, part)
    for d in (-1, 1):
        pass_on(ghost(d, d, OWN), d, d)
    features_part(4)
    for d in (-1, 1):
        for part in (0, 1):
            await_ghost(d, -d, OWN, part)
        pass_on(ghost(d, -d, OWN), d, -d)
    gather_step()
    for number in range(5, 8):
        features_part(number)

    ghosts[code(0, 0, 0)] = dom[...]
    rows = row_ids((8, WIDTH))
    for dx in SIDES:
        for dy in SIDES:
            for dz in SIDES:
                shifts[code(dx, dy, dz)] = jnp.where(
                    rows == 0,
                    dx - 0.5,
                    jnp.where(rows == 1, dy - 0.5, jnp.where(rows == 2, dz - 0.5, 0.0)),
                )
    loads[2].wait()
    lax.fori_loop(0, BLOCKS, nodes_of, 0, unroll=2)
    gather_step()
    lines = [raw[3 + k] for k in range(3)]
    length = 0.5 * jnp.sqrt(lines[0] * lines[0] + lines[1] * lines[1] + lines[2] * lines[2])
    values[0] = head(length)
    values[1] = length - head(length)
    sums = node_sums(nodes, node_hot, values, 1)
    node_len[...] = jnp.maximum(sums[0:32] + sums[32:64], DRAG_FLOOR)
    for load in loads[3:]:
        load.wait()

    for part in (0, 1):
        for dy in (-1, 1):
            await_ghost(0, dy, OFF, part)
        for d in (-1, 1):
            await_ghost(d, -d, OFF, part)
            await_ghost(d, d, OFF, part)
    for dx in SIDES:
        for dy in SIDES:
            await_ghost(dx, dy, ON)

    def pair_part(first, last):
        def body(group, carry):
            pair_group(
                group, blocks, codes, dom, ghosts, shifts, feats, weights_rows, own_out, peer_out, UNROLL
            )
            return carry

        lax.fori_loop(first // UNROLL, last // UNROLL, body, 0)

    pair_part(0, 64)
    gather_step()
    pair_part(64, SLOTS)

    live = count[0]
    table = slot_table(peer_out, live)
    code_row = code_ids[...]
    side = (code_row * 43) >> 7
    away_z = code_row - 3 * side - 1
    role_row = jnp.where(away_z == 0, OWN, jnp.where(away_z == toward, ON, OFF))
    targets = (role_row * 9 + side) * BLOCKS + block_ids[1:2, :]
    reacts = []

    def send_react(source, target_ref, target, number):
        copy = pltpu.make_async_remote_copy(
            src_ref=source,
            dst_ref=target_ref,
            send_sem=react_send.at[number],
            recv_sem=react_recv.at[number],
            device_id=target,
            device_id_type=MESH,
        )
        copy.start()
        reacts.append(copy)

    react[ON] = dot(slot_hot(targets, 288, 288), table)
    send_react(react.at[ON], from_on, device(0, 0, ON), 0)
    react[OFF] = dot(slot_hot(targets, 576, 288), table)
    for dx in SIDES:
        for dy in SIDES:
            d = ghost_slot(dx, dy, 0)
            send_react(
                react.at[OFF, pl.ds(32 * d, 32)], from_off.at[pl.ds(32 * d, 32)], device(dx, dy, OFF), 1 + d
            )
    react[OWN] = dot(slot_hot(targets, 0, 288), table)
    reacts[0].wait_recv()
    react[OWN] = react[OWN] + from_on[...]
    sent = [(dx, dy) for dx in SIDES for dy in SIDES if (dx, dy) != (0, 0)]
    for number, (dx, dy) in enumerate(sent):
        d = ghost_slot(dx, dy, 0)
        send_react(
            react.at[OWN, pl.ds(32 * d, 32)], from_layer.at[number], device(dx, dy, OWN), 10 + number
        )

    near = dot(slot_hot(block_ids[0:1, :], 0, BLOCKS), slot_table(own_out, live))
    near = near + react[OWN, pl.ds(128, 32), :]

    for _ in steps:
        pass
    sides = []
    for a in range(3):
        held = group_xy[:, :, 8 * a : 8 * a + 8, :].reshape(256, WIDTH)
        first = held.astype(BF16)
        second = (held - first.astype(F32)).astype(BF16)
        sides.append(jnp.concatenate([first, second, first], axis=0))
    spread = dot(far_table[...], jnp.concatenate(sides, axis=1))
    source = lax.broadcasted_iota(jnp.int32, (256, 384), 0) >> 4
    lane = lax.broadcasted_iota(jnp.int32, (256, 384), 1) & 15
    spread = jnp.where(source == lane, spread, 0.0)
    folded = spread[0:16]
    for k in range(1, 16):
        folded = folded + spread[16 * k : 16 * k + 16]
    folded = jnp.concatenate([folded, jnp.zeros((112, 384), F32)], axis=0)
    first = folded.astype(BF16)
    second = (folded - first.astype(F32)).astype(BF16)
    field = dot_nt(fold[...], jnp.concatenate([first, second], axis=1))
    cell = cells[...]
    hits = [cell == m for m in range(CELL_DEV)]
    per_seg = []
    for m in range(9):
        held = jnp.zeros((BLOCKS, WIDTH), F32)
        for k in range(CELL_DEV):
            held = jnp.where(hits[k], field[m : m + 1, k : k + 1], held)
        per_seg.append(held)
    burgers = [raw[6], raw[7], raw[8]]
    lines = [raw[3 + k] for k in range(3)]
    pulled = [sum(per_seg[3 * a + k] * burgers[k] for k in range(3)) for a in range(3)]
    force = [
        pulled[1] * lines[2] - pulled[2] * lines[1],
        pulled[2] * lines[0] - pulled[0] * lines[2],
        pulled[0] * lines[1] - pulled[1] * lines[0],
    ]

    for copy in reacts[1:]:
        copy.wait_recv()
    for number in range(8):
        near = near + from_layer[number]
    for d in range(9):
        near = near + from_off[pl.ds(32 * d, 32), :]
    for c in range(3):
        half = 0.5 * (force[c] + near[:, 128 * c : 128 * c + 128])
        values[c] = head(half)
        values[3 + c] = half - head(half)
    sums = node_sums(nodes, node_hot, values, 3)
    for c in range(3):
        out[c] = (sums[32 * c : 32 * c + 32] + sums[96 + 32 * c : 128 + 32 * c]) / node_len[...]

    for copy in halo + gathers + reacts:
        copy.wait_send()


def shards(seg_state, seg_cells, seg_nodes, pair_blocks, pair_offsets, pair_count):
    far_table, fold = far_tables()
    anywhere = pl.BlockSpec(memory_space=pltpu.HBM)
    out = pl.pallas_call(
        kernel,
        out_shape=jax.ShapeDtypeStruct((3, BLOCKS, WIDTH), F32),
        in_specs=[anywhere] * 5 + [pl.BlockSpec(memory_space=pltpu.SMEM)] + [anywhere] * 2,
        out_specs=pl.BlockSpec(memory_space=pltpu.VMEM),
        scratch_shapes=[
            pltpu.VMEM((9, BLOCKS, WIDTH), F32),
            pltpu.VMEM((BLOCKS, WIDTH), jnp.int32),
            pltpu.VMEM((2, BLOCKS * WIDTH), jnp.int32),
            pltpu.VMEM((2, SLOTS), jnp.int32),
            pltpu.VMEM((1, SLOTS), jnp.int32),
            pltpu.SMEM((2, SLOTS), jnp.int32),
            pltpu.SMEM((1, SLOTS), jnp.int32),
            pltpu.VMEM(far_table.shape, BF16),
            pltpu.VMEM(fold.shape, BF16),
            pltpu.VMEM((TILES, 8, WIDTH), F32),
            pltpu.VMEM((27, TILES, 8, WIDTH), F32),
            pltpu.VMEM((27, 8, WIDTH), F32),
            pltpu.VMEM((BLOCKS, 128, WIDTH), BF16),
            pltpu.VMEM((BLOCKS, 16, 256), BF16),
            pltpu.VMEM((SLOTS, 8, WIDTH), F32),
            pltpu.VMEM((SLOTS, 8, WIDTH), F32),
            pltpu.VMEM((3, 288, 384), F32),
            pltpu.VMEM((288, 384), F32),
            pltpu.VMEM((288, 384), F32),
            pltpu.VMEM((8, 32, 384), F32),
            pltpu.VMEM((BLOCKS, 128, 256), BF16),
            pltpu.VMEM((32, WIDTH), F32),
            pltpu.VMEM((6, BLOCKS, WIDTH), F32),
            pltpu.VMEM((64, WIDTH), F32),
            pltpu.VMEM((4, 8, 24, WIDTH), F32),
            pltpu.SemaphoreType.DMA((9,)),
            pltpu.SemaphoreType.DMA((43,)),
            pltpu.SemaphoreType.DMA((54,)),
            pltpu.SemaphoreType.DMA((18,)),
            pltpu.SemaphoreType.DMA((18,)),
            pltpu.SemaphoreType.DMA((13,)),
            pltpu.SemaphoreType.DMA((13,)),
        ],
        compiler_params=pltpu.CompilerParams(
            collective_id=0, has_side_effects=True, vmem_limit_bytes=62 * 1024 * 1024
        ),
    )(
        jnp.transpose(seg_state[0, 0, 0], (1, 0, 2)),
        seg_cells[0, 0, 0],
        seg_nodes[0, 0, 0],
        pair_blocks[0, 0, 0],
        pair_offsets[0, 0],
        pair_count.reshape(1),
        jnp.asarray(far_table),
        jnp.asarray(fold),
    )
    return out.reshape(1, 1, 1, 3, BLOCKS * WIDTH)


def solution(mesh):
    placed = (
        P("gx", "gy", "gz", None, None, None),
        P("gx", "gy", "gz", None, None),
        P("gx", "gy", "gz", None, None),
        P("gx", "gy", "gz", None, None),
        P("gx", "gy", "gz", None),
        P("gx", "gy", "gz"),
    )
    return jax.shard_map(
        shards,
        mesh=mesh,
        in_specs=placed,
        out_specs=P("gx", "gy", "gz", None, None),
        check_vma=False,
    )
```

```python
import jax
import jax.numpy as jnp
import ml_dtypes
import numpy as np
from jax import lax
from jax.experimental import pallas as pl
from jax.experimental.pallas import tpu as pltpu
from jax.sharding import PartitionSpec as P

CELLS = 16
PAIR_STRENGTH = 0.1
CORE_SQUARED = 0.2
FAR_STRENGTH = 0.008
DRAG_FLOOR = 0.5

BLOCKS = 32
WIDTH = 128
SLOTS = 128
TILES = 36
CELL_DEV = 16
UNROLL = 16
SIDES = (-1, 0, 1)
F32 = jnp.float32
BF16 = jnp.bfloat16
MESH = pl.DeviceIdType.MESH
NT = (((1,), (1,)), ((), ()))
PAIR_SCALE = float(PAIR_STRENGTH * (1.0 / CORE_SQUARED) ** 1.5)
OWN, ON, OFF = 0, 1, 2


def ghost_slot(dx, dy, role):
    return role * 9 + (dx + 1) * 3 + dy + 1


def dot(first, second):
    return jnp.dot(first, second, preferred_element_type=F32)


def dot_nt(first, second):
    return lax.dot_general(first, second, NT, preferred_element_type=F32)


def head(value):
    return value.astype(BF16).astype(F32)


def pair16(low, high):
    return jnp.concatenate([low, high], axis=0).astype(BF16)


def row_ids(shape):
    return lax.broadcasted_iota(jnp.int32, shape, 0)


def block_rows(tile, last, rows):
    turned = pltpu.roll(tile, 5, 0)
    line = jnp.where(rows < 3, turned, tile)
    burgers = jnp.where(rows < 2, pltpu.roll(tile, 2, 0), turned)
    burgers = jnp.where((rows == 2) | (rows == 5), last, burgers)
    return line, burgers


def outer_rows(first, second, rows):
    low = jnp.where(rows < 3, first[0:1], first[1:2]) * second
    low = jnp.where(rows < 6, low, 0.0)
    high = jnp.where(rows < 3, first[2:3] * second, 0.0)
    return low, high


def dist_rows(place, norm_row, one_row, rows):
    return jnp.where(rows < 3, place, jnp.where(rows == 3, norm_row, jnp.where(rows == 4, one_row, 0.0)))


def prepare_block(i, dom, feats, weights_rows):
    rows = row_ids((8, WIDTH))
    tile = dom[i]
    last = dom[32 + (i >> 3), pl.ds(i & 7, 1), :]
    line, burgers = block_rows(tile, last, rows)
    place = jnp.where(rows < 3, tile - 0.5, 0.0)
    norm = jnp.sum(place * place, axis=0, keepdims=True)
    scale = 1.0 / CORE_SQUARED
    outer = jnp.concatenate(outer_rows(line, burgers, rows), axis=0)
    outer_1 = head(outer)
    dist = dist_rows(-2.0 * scale * place, scale, scale * norm + 1.0, rows)
    first = head(dist)
    second = head(dist - first)
    third = head(dist - first - second)
    gap = jnp.zeros((16, WIDTH), F32)
    stack = jnp.concatenate(
        [outer_1, outer_1, outer - outer_1, gap, first, first, first, second, second, third, gap], axis=0
    )
    turned = jnp.transpose(stack).astype(BF16)
    feats[i] = turned
    place_first = head(place)
    ones = jnp.where(rows == 3, 1.0, 0.0)
    held = pair16(place_first + ones, place - place_first)
    weights_rows[i] = jnp.concatenate([held, held], axis=1)


def pair_group(group, blocks, codes, dom, ghosts, shifts, feats, weights_rows, own_out, peer_out, unroll):
    rows = row_ids((8, WIDTH))
    centre = jnp.where(rows < 3, 0.5, 0.0)
    ones = jnp.where(rows == 3, 1.0, 0.0)
    loaded = []
    for u in range(unroll):
        slot = group * unroll + u
        i = blocks[0, slot]
        g = codes[0, slot]
        j = blocks[1, slot]
        tile = ghosts[g, j]
        last = ghosts[g, 32 + (j >> 3), pl.ds(j & 7, 1), :]
        line, burgers = block_rows(tile, last, rows)
        place = jnp.where(rows < 3, tile + shifts[g], 0.0)
        norm = jnp.sum(place * place, axis=0, keepdims=True)
        same = jnp.concatenate(outer_rows(line, burgers, rows), axis=0)
        crossed = jnp.concatenate(outer_rows(burgers, line, rows), axis=0)
        same_1 = same.astype(BF16)
        same_2 = (same - same_1.astype(F32)).astype(BF16)
        crossed_1 = crossed.astype(BF16)
        crossed_2 = (crossed - crossed_1.astype(F32)).astype(BF16)
        top = jnp.concatenate([same_1, crossed_1], axis=1)
        products = jnp.concatenate([top, jnp.concatenate([same_2, crossed_2], axis=1), top], axis=0)
        dist = dist_rows(place, norm, 1.0, rows)
        first = head(dist)
        rest = dist - first
        second = head(rest)
        dists = jnp.concatenate(
            [
                jnp.zeros((64, WIDTH), BF16),
                pair16(first, second),
                pair16(rest - second, first),
                pair16(second, first),
                jnp.zeros((16, WIDTH), BF16),
            ],
            axis=0,
        )
        place_1 = jnp.where(rows < 3, first, 0.0)
        held = pair16(place_1 + ones, place - place_1)
        held = jnp.concatenate([held, held], axis=1)
        loaded.append((slot, i, place, products, dists, held))
    outs = []
    for slot, i, place, products, dists, held in loaded:
        feat = feats[i]
        outs.append((dot(feat[:, :48], products), dot(feat, dists)))
    strengths = []
    for both, dist in outs:
        inv = lax.rsqrt(dist)
        inv_sq = inv * inv
        strength = (inv_sq * inv) * (both[:, 0:128] + both[:, 128:256] * inv_sq)
        high = strength.astype(BF16)
        low = (strength - high.astype(F32)).astype(BF16)
        strengths.append((high, low))
    for (slot, i, place, products, dists, held), (high, low) in zip(loaded, strengths):
        peer = dot(weights_rows[i], jnp.concatenate([high, low], axis=0))
        own = dot_nt(held, jnp.concatenate([high, low], axis=1))
        peer = peer[0:8] + peer[8:16]
        own = own[0:8] + own[8:16]
        home = dom[i] - centre
        own_out[slot] = home * own[3:4] - own
        peer_out[slot] = place * peer[3:4] - peer


def slot_table(slot_out, live):
    keep = row_ids((SLOTS, WIDTH)) < live
    parts = [
        jnp.where(keep, PAIR_SCALE * slot_out[:, c, :], 0.0) for c in range(3)
    ]
    table = jnp.concatenate(parts, axis=1)
    first = table.astype(BF16)
    return jnp.concatenate([first, (table - first.astype(F32)).astype(BF16)], axis=0)


def slot_hot(targets, base, count):
    ids = row_ids((count, SLOTS)) + base
    hot = jnp.where(ids == targets, 1.0, 0.0).astype(BF16)
    return jnp.concatenate([hot, hot], axis=1)


def moment_block(b, dom, cells, total):
    rows = row_ids((8, WIDTH))
    tile = dom[b]
    last = dom[32 + (b >> 3), pl.ds(b & 7, 1), :]
    line, burgers = block_rows(tile, last, rows)
    hot = row_ids((CELL_DEV, WIDTH)) == cells[pl.ds(b, 1), :]
    line_1 = head(line)
    line_2 = line - line_1
    burgers = jnp.where(rows < 3, burgers, 0.0)
    burgers_1 = head(burgers)
    burgers_2 = burgers - burgers_1
    zero = jnp.zeros((CELL_DEV, WIDTH), F32)
    spread = [
        jnp.concatenate([jnp.where(hot, part[k : k + 1], zero) for k in range(3)], axis=0).astype(BF16)
        for part in (line_1, line_2)
    ]
    pad = jnp.zeros((8, WIDTH), F32)
    left = jnp.concatenate([pair16(burgers_1, pad), pair16(burgers_1, pad), pair16(burgers_2, pad)], axis=1)
    right = jnp.concatenate([spread[0], spread[1], spread[0]], axis=1)
    return total + dot_nt(left, right)


def nodes_row(nodes, e, b):
    return nodes[e : e + 1, pl.ds(pl.multiple_of(b * WIDTH, WIDTH), WIDTH)]


def node_onehot(b, nodes, node_hot):
    lows = [
        jnp.where(row_ids((128, WIDTH)) == (nodes_row(nodes, e, b) & 127), 1.0, 0.0).astype(BF16)
        for e in range(2)
    ]
    node_hot[b] = jnp.concatenate(lows, axis=1)


def node_sums(nodes, node_hot, values, count):
    together = 4

    def body(turn, total):
        parts, hots = [], []
        for u in range(together):
            b = turn * together + u
            for e in range(2):
                hit = row_ids((32, WIDTH)) == nodes_row(nodes, e, b) >> 7
                rows = [jnp.where(hit, values[c, pl.ds(b, 1), :], 0.0) for c in range(2 * count)]
                parts.append(jnp.concatenate(rows, axis=0).astype(BF16))
            hots.append(node_hot[b])
        return total + dot_nt(jnp.concatenate(parts, axis=1), jnp.concatenate(hots, axis=1))

    return lax.fori_loop(0, BLOCKS // together, body, jnp.zeros((64 * count, WIDTH), F32))


def far_tables():
    index = np.arange(CELL_DEV)
    inner = np.stack([index // 4, index // 2 % 2, index % 2])
    rel = np.arange(256)
    away = np.stack([rel // 64 * 4, (rel // 8 % 8 - 1) * 2, (rel % 8 - 1) * 2])
    delta = away[:, None, None, :] + inner[:, :, None, None] - inner[:, None, :, None]
    delta = (delta + 8) % 16 - 8
    dist = np.sqrt(np.maximum((delta.astype(np.float64) ** 2).sum(0), 1.0))
    far = np.where(np.abs(delta).max(0) > 1, FAR_STRENGTH / dist, 0.0).astype(np.float32)
    far = far.reshape(256, 256)
    first = far.astype(ml_dtypes.bfloat16)
    second = (far - first.astype(np.float32)).astype(ml_dtypes.bfloat16)
    table = np.concatenate([first, first, second], axis=1)
    lanes = np.arange(384)
    part = lanes % 128
    fold = np.zeros((16, 384), np.float32)
    for lane in lanes[part < 48]:
        fold[3 * (lane // 128) + part[lane] // 16, lane] = 1.0
    fold = np.concatenate([fold, fold], axis=1).astype(ml_dtypes.bfloat16)
    return table, fold


def kernel(
    state_in, cells_in, nodes_in, blocks_in, codes_in, count, far_in, fold_in, out,
    raw, cells, nodes, block_ids, code_ids, blocks, codes, far_table, fold,
    dom, ghosts, shifts, feats, weights_rows, own_out, peer_out, react, from_on, from_off, from_layer,
    node_hot, node_len, values, group_z, group_xy,
    load_sem, halo_send, halo_recv, react_send, react_recv, gather_send, gather_recv,
):
    size_x, size_y, size_z = 4, 8, 8
    me_x = lax.axis_index("gx")
    me_y = lax.axis_index("gy")
    me_z = lax.axis_index("gz")
    toward = 1 - 2 * lax.rem(me_z, 2)

    loads = [
        pltpu.make_async_copy(source, target, load_sem.at[number])
        for number, (source, target) in enumerate(
            [
                (state_in, raw), (cells_in, cells), (nodes_in, nodes), (blocks_in, blocks), (codes_in, codes),
                (blocks_in, block_ids), (codes_in, code_ids), (far_in, far_table), (fold_in, fold),
            ]
        )
    ]
    for load in loads:
        load.start()

    def at_x(d):
        return lax.rem(me_x + d + size_x, size_x)

    def at_y(d):
        return lax.rem(me_y + d + size_y, size_y)

    def at_z(d):
        return lax.rem(me_z + d + size_z, size_z)

    def away(role):
        return 0 if role == OWN else (toward if role == ON else -toward)

    def device(dx, dy, role):
        return (at_x(dx), at_y(dy), at_z(away(role)))

    def code(dx, dy, dz):
        return (dx + 1) * 9 + (dy + 1) * 3 + dz + 1

    peers = [
        device(-1, 0, OWN), device(1, 0, OWN), device(0, -1, OWN), device(0, 1, OWN), device(0, 0, OFF), device(0, 0, ON)
    ]
    barrier = pltpu.get_barrier_semaphore()
    for peer in peers:
        pl.semaphore_signal(barrier, inc=1, device_id=peer, device_id_type=MESH)
    loads[0].wait()
    for k in range(8):
        dom[0:BLOCKS, k, :] = raw[k]
    dom[BLOCKS:TILES] = raw[8].reshape(4, 8, WIDTH)
    pl.semaphore_wait(barrier, len(peers))

    halo = []
    half = TILES // 2

    def piece(ref, part):
        return ref if part is None else ref.at[pl.ds(part * half, half)]

    def ghost(dx, dy, role):
        return ghosts.at[code(dx, dy, away(role))]

    def send_ghost(source, to, slot, offset, part):
        copy = pltpu.make_async_remote_copy(
            src_ref=piece(source, part),
            dst_ref=piece(ghosts.at[code(*offset)], part),
            send_sem=halo_send.at[len(halo)],
            recv_sem=halo_recv.at[2 * slot + (part or 0)],
            device_id=device(*to),
            device_id_type=MESH,
        )
        copy.start()
        halo.append(copy)

    def await_ghost(dx, dy, role, part=None):
        pltpu.make_async_remote_copy(
            src_ref=piece(dom, part),
            dst_ref=piece(ghost(dx, dy, role), part),
            send_sem=halo_send.at[0],
            recv_sem=halo_recv.at[2 * ghost_slot(dx, dy, role) + (part or 0)],
            device_id=device(0, 0, ON),
            device_id_type=MESH,
        ).wait_recv()

    def pass_x(source, e, dy, role, part):
        send_ghost(source, (e, 0, OWN), ghost_slot(-e, dy, role), (-e, dy, away(role)), part)

    def pass_y(source, e, dx, role, part):
        send_ghost(source, (0, e, OWN), ghost_slot(dx, -e, role), (dx, -e, away(role)), part)

    def pass_off(source, dx, dy, part):
        send_ghost(source, (0, 0, OFF), ghost_slot(dx, dy, OFF), (dx, dy, toward), part)

    def pass_on(source, dx, dy):
        send_ghost(source, (0, 0, ON), ghost_slot(dx, dy, ON), (dx, dy, -toward), None)

    for part in (0, 1):
        for e in (-1, 1):
            pass_y(dom, e, 0, OWN, part)
        for e in (-1, 1):
            pass_x(dom, e, 0, OWN, part)
        pass_off(dom, 0, 0, part)
    pass_on(dom, 0, 0)

    gathers = []

    def gather(source, target, to):
        number = len(gathers)
        copy = pltpu.make_async_remote_copy(
            src_ref=source,
            dst_ref=target,
            send_sem=gather_send.at[number],
            recv_sem=gather_recv.at[number],
            device_id=to,
            device_id_type=MESH,
        )
        copy.start()
        gathers.append(copy)
        return copy

    def spread_of_8(ref_of, at):
        for distance, moves in ((1, ((1, 2, 1, -1), (1, 0, 1, 1))), (3, ((0, 3, 3, -1), (1, 6, 2, 1)))):
            sent = [
                gather(ref_of(first, count), ref_of(target, count), at(sign * distance))
                for first, target, count, sign in moves
            ]
            yield
            for copy in sent:
                copy.wait_recv()

    def gather_steps():
        yield from spread_of_8(
            lambda first, count: group_z.at[pl.ds(8 * first, 8 * count)], lambda d: (me_x, me_y, at_z(d))
        )
        for a in range(3):
            group_xy[0, 1, 8 * a : 8 * a + 8, :] = group_z[pl.ds(a, 8, stride=8), :]
        yield from spread_of_8(
            lambda first, count: group_xy.at[0, pl.ds(first, count)], lambda d: (me_x, at_y(d), me_z)
        )
        sent = [
            gather(group_xy.at[0], group_xy.at[r], (at_x(-r), me_y, me_z)) for r in range(1, size_x)
        ]
        yield
        for copy in sent:
            copy.wait_recv()

    steps = gather_steps()

    def gather_step():
        next(steps, None)

    def features(b, carry):
        prepare_block(b, dom, feats, weights_rows)
        return carry

    def features_part(number):
        lax.fori_loop(4 * number, 4 * number + 4, features, 0, unroll=2)

    def nodes_of(b, carry):
        node_onehot(b, nodes, node_hot)
        return carry

    loads[1].wait()
    moments = lax.fori_loop(
        0, BLOCKS, lambda b, total: moment_block(b, dom, cells, total), jnp.zeros((16, 48), F32), unroll=4
    )
    group_z[8:16, :] = jnp.concatenate([moments[0:8], jnp.zeros((8, 80), F32)], axis=1)

    for part in (0, 1):
        await_ghost(0, 0, OFF, part)
        for e in (-1, 1):
            pass_x(ghost(0, 0, OFF), e, 0, OFF, part)
    await_ghost(0, 0, ON)
    gather_step()
    features_part(0)
    for part in (0, 1):
        for dx in (-1, 1):
            await_ghost(dx, 0, OWN, part)
            pass_y(ghost(dx, 0, OWN), -dx, dx, OWN, part)
    for dx in (-1, 1):
        pass_on(ghost(dx, 0, OWN), dx, 0)
    features_part(1)
    for part in (0, 1):
        for dy in (-1, 1):
            await_ghost(0, dy, OWN, part)
            pass_x(ghost(0, dy, OWN), dy, dy, OWN, part)
            pass_off(ghost(0, dy, OWN), 0, dy, part)
    for dy in (-1, 1):
        pass_on(ghost(0, dy, OWN), 0, dy)
    gather_step()
    features_part(2)
    for part in (0, 1):
        for dx in (-1, 1):
            await_ghost(dx, 0, OFF, part)
            pass_y(ghost(dx, 0, OFF), dx, dx, OFF, part)
    features_part(3)
    for part in (0, 1):
        for d in (-1, 1):
            await_ghost(d, d, OWN, part)
            pass_off(ghost(d, d, OWN), d, d, part)
    for d in (-1, 1):
        pass_on(ghost(d, d, OWN), d, d)
    features_part(4)
    for d in (-1, 1):
        for part in (0, 1):
            await_ghost(d, -d, OWN, part)
        pass_on(ghost(d, -d, OWN), d, -d)
    gather_step()
    for number in range(5, 8):
        features_part(number)

    ghosts[code(0, 0, 0)] = dom[...]
    rows = row_ids((8, WIDTH))
    for dx in SIDES:
        for dy in SIDES:
            for dz in SIDES:
                shifts[code(dx, dy, dz)] = jnp.where(
                    rows == 0,
                    dx - 0.5,
                    jnp.where(rows == 1, dy - 0.5, jnp.where(rows == 2, dz - 0.5, 0.0)),
                )
    loads[2].wait()
    lax.fori_loop(0, BLOCKS, nodes_of, 0, unroll=2)
    lines = [raw[3 + k] for k in range(3)]
    length = 0.5 * jnp.sqrt(lines[0] * lines[0] + lines[1] * lines[1] + lines[2] * lines[2])
    values[0] = head(length)
    values[1] = length - head(length)
    sums = node_sums(nodes, node_hot, values, 1)
    node_len[...] = jnp.maximum(sums[0:32] + sums[32:64], DRAG_FLOOR)
    for load in loads[3:]:
        load.wait()

    for part in (0, 1):
        for dy in (-1, 1):
            await_ghost(0, dy, OFF, part)
        for d in (-1, 1):
            await_ghost(d, -d, OFF, part)
            await_ghost(d, d, OFF, part)
    for dx in SIDES:
        for dy in SIDES:
            if (dx, dy) != (0, 0):
                await_ghost(dx, dy, ON)

    def pair_part(first, last):
        def body(group, carry):
            pair_group(
                group, blocks, codes, dom, ghosts, shifts, feats, weights_rows, own_out, peer_out, UNROLL
            )
            return carry

        lax.fori_loop(first // UNROLL, last // UNROLL, body, 0)

    gather_step()
    pair_part(0, 64)
    gather_step()
    pair_part(64, SLOTS)

    live = count[0]
    table = slot_table(peer_out, live)
    code_row = code_ids[...]
    side = (code_row * 43) >> 7
    away_z = code_row - 3 * side - 1
    role_row = jnp.where(away_z == 0, OWN, jnp.where(away_z == toward, ON, OFF))
    targets = (role_row * 9 + side) * BLOCKS + block_ids[1:2, :]
    reacts = []

    def send_react(source, target_ref, target, number):
        copy = pltpu.make_async_remote_copy(
            src_ref=source,
            dst_ref=target_ref,
            send_sem=react_send.at[number],
            recv_sem=react_recv.at[number],
            device_id=target,
            device_id_type=MESH,
        )
        copy.start()
        reacts.append(copy)

    react[ON] = dot(slot_hot(targets, 288, 288), table)
    send_react(react.at[ON], from_on, device(0, 0, ON), 0)
    react[OFF] = dot(slot_hot(targets, 576, 288), table)
    for dx in SIDES:
        for dy in SIDES:
            d = ghost_slot(dx, dy, 0)
            send_react(
                react.at[OFF, pl.ds(32 * d, 32)], from_off.at[pl.ds(32 * d, 32)], device(dx, dy, OFF), 1 + d
            )
    react[OWN] = dot(slot_hot(targets, 0, 288), table)
    reacts[0].wait_recv()
    react[OWN] = react[OWN] + from_on[...]
    sent = [(dx, dy) for dx in SIDES for dy in SIDES if (dx, dy) != (0, 0)]
    for number, (dx, dy) in enumerate(sent):
        d = ghost_slot(dx, dy, 0)
        send_react(
            react.at[OWN, pl.ds(32 * d, 32)], from_layer.at[number], device(dx, dy, OWN), 10 + number
        )

    near = dot(slot_hot(block_ids[0:1, :], 0, BLOCKS), slot_table(own_out, live))
    near = near + react[OWN, pl.ds(128, 32), :]

    for _ in steps:
        pass
    sides = []
    for a in range(3):
        held = group_xy[:, :, 8 * a : 8 * a + 8, :].reshape(256, WIDTH)
        first = held.astype(BF16)
        second = (held - first.astype(F32)).astype(BF16)
        sides.append(jnp.concatenate([first, second, first], axis=0))
    spread = dot(far_table[...], jnp.concatenate(sides, axis=1))
    source = lax.broadcasted_iota(jnp.int32, (256, 384), 0) >> 4
    lane = lax.broadcasted_iota(jnp.int32, (256, 384), 1) & 15
    spread = jnp.where(source == lane, spread, 0.0)
    folded = spread[0:16]
    for k in range(1, 16):
        folded = folded + spread[16 * k : 16 * k + 16]
    folded = jnp.concatenate([folded, jnp.zeros((112, 384), F32)], axis=0)
    first = folded.astype(BF16)
    second = (folded - first.astype(F32)).astype(BF16)
    field = dot_nt(fold[...], jnp.concatenate([first, second], axis=1))
    cell = cells[...]
    hits = [cell == m for m in range(CELL_DEV)]
    per_seg = []
    for m in range(9):
        held = jnp.zeros((BLOCKS, WIDTH), F32)
        for k in range(CELL_DEV):
            held = jnp.where(hits[k], field[m : m + 1, k : k + 1], held)
        per_seg.append(held)
    burgers = [raw[6], raw[7], raw[8]]
    lines = [raw[3 + k] for k in range(3)]
    pulled = [sum(per_seg[3 * a + k] * burgers[k] for k in range(3)) for a in range(3)]
    force = [
        pulled[1] * lines[2] - pulled[2] * lines[1],
        pulled[2] * lines[0] - pulled[0] * lines[2],
        pulled[0] * lines[1] - pulled[1] * lines[0],
    ]

    for copy in reacts[1:]:
        copy.wait_recv()
    for number in range(8):
        near = near + from_layer[number]
    for d in range(9):
        near = near + from_off[pl.ds(32 * d, 32), :]
    for c in range(3):
        half = 0.5 * (force[c] + near[:, 128 * c : 128 * c + 128])
        values[c] = head(half)
        values[3 + c] = half - head(half)
    sums = node_sums(nodes, node_hot, values, 3)
    for c in range(3):
        out[c] = (sums[32 * c : 32 * c + 32] + sums[96 + 32 * c : 128 + 32 * c]) / node_len[...]

    for copy in halo + gathers + reacts:
        copy.wait_send()


def shards(seg_state, seg_cells, seg_nodes, pair_blocks, pair_offsets, pair_count):
    far_table, fold = far_tables()
    anywhere = pl.BlockSpec(memory_space=pltpu.HBM)
    out = pl.pallas_call(
        kernel,
        out_shape=jax.ShapeDtypeStruct((3, BLOCKS, WIDTH), F32),
        in_specs=[anywhere] * 5 + [pl.BlockSpec(memory_space=pltpu.SMEM)] + [anywhere] * 2,
        out_specs=pl.BlockSpec(memory_space=pltpu.VMEM),
        scratch_shapes=[
            pltpu.VMEM((9, BLOCKS, WIDTH), F32),
            pltpu.VMEM((BLOCKS, WIDTH), jnp.int32),
            pltpu.VMEM((2, BLOCKS * WIDTH), jnp.int32),
            pltpu.VMEM((2, SLOTS), jnp.int32),
            pltpu.VMEM((1, SLOTS), jnp.int32),
            pltpu.SMEM((2, SLOTS), jnp.int32),
            pltpu.SMEM((1, SLOTS), jnp.int32),
            pltpu.VMEM(far_table.shape, BF16),
            pltpu.VMEM(fold.shape, BF16),
            pltpu.VMEM((TILES, 8, WIDTH), F32),
            pltpu.VMEM((27, TILES, 8, WIDTH), F32),
            pltpu.VMEM((27, 8, WIDTH), F32),
            pltpu.VMEM((BLOCKS, 128, WIDTH), BF16),
            pltpu.VMEM((BLOCKS, 16, 256), BF16),
            pltpu.VMEM((SLOTS, 8, WIDTH), F32),
            pltpu.VMEM((SLOTS, 8, WIDTH), F32),
            pltpu.VMEM((3, 288, 384), F32),
            pltpu.VMEM((288, 384), F32),
            pltpu.VMEM((288, 384), F32),
            pltpu.VMEM((8, 32, 384), F32),
            pltpu.VMEM((BLOCKS, 128, 256), BF16),
            pltpu.VMEM((32, WIDTH), F32),
            pltpu.VMEM((6, BLOCKS, WIDTH), F32),
            pltpu.VMEM((64, WIDTH), F32),
            pltpu.VMEM((4, 8, 24, WIDTH), F32),
            pltpu.SemaphoreType.DMA((9,)),
            pltpu.SemaphoreType.DMA((43,)),
            pltpu.SemaphoreType.DMA((54,)),
            pltpu.SemaphoreType.DMA((18,)),
            pltpu.SemaphoreType.DMA((18,)),
            pltpu.SemaphoreType.DMA((11,)),
            pltpu.SemaphoreType.DMA((11,)),
        ],
        compiler_params=pltpu.CompilerParams(
            collective_id=0, has_side_effects=True, vmem_limit_bytes=62 * 1024 * 1024
        ),
    )(
        jnp.transpose(seg_state[0, 0, 0], (1, 0, 2)),
        seg_cells[0, 0, 0],
        seg_nodes[0, 0, 0],
        pair_blocks[0, 0, 0],
        pair_offsets[0, 0],
        pair_count.reshape(1),
        jnp.asarray(far_table),
        jnp.asarray(fold),
    )
    return out.reshape(1, 1, 1, 3, BLOCKS * WIDTH)


def solution(mesh):
    placed = (
        P("gx", "gy", "gz", None, None, None),
        P("gx", "gy", "gz", None, None),
        P("gx", "gy", "gz", None, None),
        P("gx", "gy", "gz", None, None),
        P("gx", "gy", "gz", None),
        P("gx", "gy", "gz"),
    )
    return jax.shard_map(
        shards,
        mesh=mesh,
        in_specs=placed,
        out_specs=P("gx", "gy", "gz", None, None),
        check_vma=False,
    )
```

```python
import jax
import jax.numpy as jnp
import ml_dtypes
import numpy as np
from jax import lax
from jax.experimental import pallas as pl
from jax.experimental.pallas import tpu as pltpu
from jax.sharding import PartitionSpec as P

CELLS = 16
PAIR_STRENGTH = 0.1
CORE_SQUARED = 0.2
FAR_STRENGTH = 0.008
DRAG_FLOOR = 0.5

BLOCKS = 32
WIDTH = 128
SLOTS = 128
TILES = 36
CELL_DEV = 16
UNROLL = 64
LAG1, LAG2, LAG3 = (2, 4, 4)
TOGETHER = 16
SIDES = (-1, 0, 1)
F32 = jnp.float32
BF16 = jnp.bfloat16
MESH = pl.DeviceIdType.MESH
NT = (((1,), (1,)), ((), ()))
PAIR_SCALE = float(PAIR_STRENGTH * (1.0 / CORE_SQUARED) ** 1.5)
OWN, ON, OFF = 0, 1, 2


def ghost_slot(dx, dy, role):
    return role * 9 + (dx + 1) * 3 + dy + 1


def dot(first, second):
    return jnp.dot(first, second, preferred_element_type=F32)


def dot_nt(first, second):
    return lax.dot_general(first, second, NT, preferred_element_type=F32)


def head(value):
    return value.astype(BF16).astype(F32)


def pair16(low, high):
    return jnp.concatenate([low, high], axis=0).astype(BF16)


def row_ids(shape):
    return lax.broadcasted_iota(jnp.int32, shape, 0)


def block_rows(tile, last, rows):
    turned = pltpu.roll(tile, 5, 0)
    line = jnp.where(rows < 3, turned, tile)
    burgers = jnp.where(rows < 2, pltpu.roll(tile, 2, 0), turned)
    burgers = jnp.where((rows == 2) | (rows == 5), last, burgers)
    return line, burgers


def outer_rows(first, second, rows):
    low = jnp.where(rows < 3, first[0:1], first[1:2]) * second
    low = jnp.where(rows < 6, low, 0.0)
    high = jnp.where(rows < 3, first[2:3] * second, 0.0)
    return low, high


def dist_rows(place, norm_row, one_row, rows):
    return jnp.where(rows < 3, place, jnp.where(rows == 3, norm_row, jnp.where(rows == 4, one_row, 0.0)))


def prepare_block(i, dom, feats, weights_rows):
    rows = row_ids((8, WIDTH))
    tile = dom[i]
    last = dom[32 + (i >> 3), pl.ds(i & 7, 1), :]
    line, burgers = block_rows(tile, last, rows)
    place = jnp.where(rows < 3, tile - 0.5, 0.0)
    norm = jnp.sum(place * place, axis=0, keepdims=True)
    scale = 1.0 / CORE_SQUARED
    same = jnp.concatenate(outer_rows(line, burgers, rows), axis=0)
    same_1 = head(same)
    crossed = jnp.concatenate(outer_rows(burgers, line, rows), axis=0)
    crossed_1 = head(crossed)
    dist = dist_rows(-2.0 * scale * place, scale, scale * norm + 1.0, rows)
    first = head(dist)
    second = head(dist - first)
    third = head(dist - first - second)
    gap = jnp.zeros((16, WIDTH), F32)
    stack = jnp.concatenate([same_1, same_1, same - same_1, gap, first, first, first, second, second, third, gap], axis=0)
    feats[i, 0:WIDTH] = jnp.transpose(stack).astype(BF16)
    stack = jnp.concatenate([crossed_1, crossed_1, crossed - crossed_1, jnp.zeros((80, WIDTH), F32)], axis=0)
    feats[i, WIDTH : 2 * WIDTH] = jnp.transpose(stack).astype(BF16)
    place_first = head(place)
    ones = jnp.where(rows == 3, 1.0, 0.0)
    held = pair16(place_first + ones, place - place_first)
    weights_rows[i] = jnp.concatenate([held, held], axis=1)


def pair_group(group, blocks, codes, dom, ghosts, shifts, feats, weights_rows, own_out, peer_out, unroll):
    rows = row_ids((8, WIDTH))
    centre = jnp.where(rows < 3, 0.5, 0.0)
    def load(u):
        slot = group * unroll + u
        i = blocks[0, slot]
        g = codes[0, slot]
        j = blocks[1, slot]
        tile = ghosts[g, j]
        last = ghosts[g, 32 + (j >> 3), pl.ds(j & 7, 1), :]
        line, burgers = block_rows(tile, last, rows)
        place = jnp.where(rows < 3, tile + shifts[g], 0.0)
        norm = jnp.sum(place * place, axis=0, keepdims=True)
        product = jnp.concatenate(outer_rows(line, burgers, rows), axis=0)
        product_1 = product.astype(BF16)
        product_2 = (product - product_1.astype(F32)).astype(BF16)
        products = jnp.concatenate([product_1, product_2, product_1], axis=0)
        dist = dist_rows(place, norm, 1.0, rows)
        first = head(dist)
        rest = dist - first
        second = head(rest)
        dists = jnp.concatenate(
            [
                jnp.zeros((64, WIDTH), BF16),
                pair16(first, second),
                pair16(rest - second, first),
                pair16(second, first),
                jnp.zeros((16, WIDTH), BF16),
            ],
            axis=0,
        )
        held = pair16(first, second)
        return slot, i, place, products, dists, held

    def multiply(slot, i, place, products, dists, held):
        return dot(feats[i][:, :48], products), dot(feats[i, 0:WIDTH], dists)

    def strength_of(both, dist):
        inv = lax.rsqrt(dist)
        inv_sq = inv * inv
        strength = (inv_sq * inv) * (both[0:128] + both[128:256] * inv_sq)
        high = strength.astype(BF16)
        return high, (strength - high.astype(F32)).astype(BF16)

    def reduce(slot, i, place, products, dists, held, high, low):
        peer = dot(weights_rows[i], jnp.concatenate([high, low], axis=0))
        own = dot_nt(jnp.concatenate([held, held], axis=1), jnp.concatenate([high, low], axis=1))
        peer = peer[0:8] + peer[8:16]
        own = own[0:8] + own[8:16]
        home = dom[i] - centre
        own_out[slot] = home * own[4:5] - own
        peer_out[slot] = place * peer[3:4] - peer

    loaded, outs, strengths = {}, {}, {}
    for turn in range(unroll + LAG1 + LAG2 + LAG3):
        if turn < unroll:
            loaded[turn] = load(turn)
        u = turn - LAG1
        if 0 <= u < unroll:
            outs[u] = multiply(*loaded[u])
        u -= LAG2
        if 0 <= u < unroll:
            strengths[u] = strength_of(*outs.pop(u))
        u -= LAG3
        if 0 <= u < unroll:
            reduce(*loaded.pop(u), *strengths.pop(u))


def slot_table(slot_out, live):
    keep = row_ids((SLOTS, WIDTH)) < live
    parts = [
        jnp.where(keep, PAIR_SCALE * slot_out[:, c, :], 0.0) for c in range(3)
    ]
    table = jnp.concatenate(parts, axis=1)
    first = table.astype(BF16)
    return jnp.concatenate([first, (table - first.astype(F32)).astype(BF16)], axis=0)


def slot_hot(targets, base, count):
    ids = row_ids((count, SLOTS)) + base
    hot = jnp.where(ids == targets, 1.0, 0.0).astype(BF16)
    return jnp.concatenate([hot, hot], axis=1)


def moment_block(b, dom, cells, total):
    rows = row_ids((8, WIDTH))
    tile = dom[b]
    last = dom[32 + (b >> 3), pl.ds(b & 7, 1), :]
    line, burgers = block_rows(tile, last, rows)
    hot = row_ids((CELL_DEV, WIDTH)) == cells[pl.ds(b, 1), :]
    line_1 = head(line)
    line_2 = line - line_1
    burgers = jnp.where(rows < 3, burgers, 0.0)
    burgers_1 = head(burgers)
    burgers_2 = burgers - burgers_1
    zero = jnp.zeros((CELL_DEV, WIDTH), F32)
    spread = [
        jnp.concatenate([jnp.where(hot, part[k : k + 1], zero) for k in range(3)], axis=0).astype(BF16)
        for part in (line_1, line_2)
    ]
    pad = jnp.zeros((8, WIDTH), F32)
    left = jnp.concatenate([pair16(burgers_1, pad), pair16(burgers_1, pad), pair16(burgers_2, pad)], axis=1)
    right = jnp.concatenate([spread[0], spread[1], spread[0]], axis=1)
    return total + dot_nt(left, right)


def node_tables(nodes, node_rows, node_hot):
    def copy_row(b, carry):
        for e in range(2):
            node_rows[e, pl.ds(b, 1), :] = nodes[e : e + 1, pl.ds(pl.multiple_of(b * WIDTH, WIDTH), WIDTH)]
        return carry

    lax.fori_loop(0, BLOCKS, copy_row, 0, unroll=4)
    lanes = lax.broadcasted_iota(jnp.int32, (WIDTH, WIDTH), 1).astype(F32)
    for e in range(2):
        lows = (node_rows[e] & 127).astype(F32)
        turned = jnp.transpose(jnp.concatenate([lows, jnp.zeros((96, WIDTH), F32)], axis=0))
        for b in range(BLOCKS):
            node_hot[b, e * WIDTH : (e + 1) * WIDTH, :] = jnp.where(turned[:, b : b + 1] == lanes, 1.0, 0.0).astype(BF16)


def node_sums(node_rows, node_hot, values, count):
    together = TOGETHER

    def body(turn, total):
        parts, hots = [], []
        for u in range(together):
            b = turn * together + u
            for e in range(2):
                hit = row_ids((32, WIDTH)) == node_rows[e, pl.ds(b, 1), :] >> 7
                rows = [jnp.where(hit, values[c, pl.ds(b, 1), :], 0.0) for c in range(2 * count)]
                parts.append(jnp.concatenate(rows, axis=0).astype(BF16))
            hots.append(node_hot[b])
        return total + dot(jnp.concatenate(parts, axis=1), jnp.concatenate(hots, axis=0))

    return lax.fori_loop(0, BLOCKS // together, body, jnp.zeros((64 * count, WIDTH), F32))


def far_tables():
    index = np.arange(CELL_DEV)
    inner = np.stack([index // 4, index // 2 % 2, index % 2])
    rel = np.arange(256)
    away = np.stack([rel // 64 * 4, (rel // 8 % 8 - 1) * 2, (rel % 8 - 1) * 2])
    delta = away[:, None, None, :] + inner[:, :, None, None] - inner[:, None, :, None]
    delta = (delta + 8) % 16 - 8
    dist = np.sqrt(np.maximum((delta.astype(np.float64) ** 2).sum(0), 1.0))
    far = np.where(np.abs(delta).max(0) > 1, FAR_STRENGTH / dist, 0.0).astype(np.float32)
    far = far.reshape(256, 256)
    first = far.astype(ml_dtypes.bfloat16)
    second = (far - first.astype(np.float32)).astype(ml_dtypes.bfloat16)
    table = np.concatenate([first, first, second], axis=1)
    lanes = np.arange(384)
    part = lanes % 128
    fold = np.zeros((16, 384), np.float32)
    for lane in lanes[part < 48]:
        fold[3 * (lane // 128) + part[lane] // 16, lane] = 1.0
    fold = np.concatenate([fold, fold], axis=1).astype(ml_dtypes.bfloat16)
    return table, fold


def kernel(
    state_in, cells_in, nodes_in, blocks_in, codes_in, count, far_in, fold_in, out,
    raw, cells, nodes, block_ids, code_ids, blocks, codes, far_table, fold,
    dom, ghosts, shifts, feats, weights_rows, own_out, peer_out, react, from_on, from_off, from_layer,
    node_rows, node_hot, node_len, values, group_z, group_xy,
    load_sem, halo_send, halo_recv, react_send, react_recv, gather_send, gather_recv,
):
    size_x, size_y, size_z = 4, 8, 8
    me_x = lax.axis_index("gx")
    me_y = lax.axis_index("gy")
    me_z = lax.axis_index("gz")
    toward = 1 - 2 * lax.rem(me_z, 2)

    loads = [
        pltpu.make_async_copy(source, target, load_sem.at[number])
        for number, (source, target) in enumerate(
            [
                (state_in, raw), (cells_in, cells), (nodes_in, nodes), (blocks_in, blocks), (codes_in, codes),
                (blocks_in, block_ids), (codes_in, code_ids), (far_in, far_table), (fold_in, fold),
            ]
        )
    ]
    for load in loads:
        load.start()

    def at_x(d):
        return lax.rem(me_x + d + size_x, size_x)

    def at_y(d):
        return lax.rem(me_y + d + size_y, size_y)

    def at_z(d):
        return lax.rem(me_z + d + size_z, size_z)

    def away(role):
        return 0 if role == OWN else (toward if role == ON else -toward)

    def device(dx, dy, role):
        return (at_x(dx), at_y(dy), at_z(away(role)))

    def code(dx, dy, dz):
        return (dx + 1) * 9 + (dy + 1) * 3 + dz + 1

    peers = [
        device(-1, 0, OWN), device(1, 0, OWN), device(0, -1, OWN), device(0, 1, OWN), device(0, 0, OFF), device(0, 0, ON)
    ]
    barrier = pltpu.get_barrier_semaphore()
    for peer in peers:
        pl.semaphore_signal(barrier, inc=1, device_id=peer, device_id_type=MESH)
    loads[0].wait()
    for k in range(8):
        dom[0:BLOCKS, k, :] = raw[k]
    dom[BLOCKS:TILES] = raw[8].reshape(4, 8, WIDTH)
    pl.semaphore_wait(barrier, len(peers))

    halo = []
    half = TILES // 2

    def piece(ref, part):
        return ref if part is None else ref.at[pl.ds(part * half, half)]

    def ghost(dx, dy, role):
        return ghosts.at[code(dx, dy, away(role))]

    def send_ghost(source, to, slot, offset, part):
        copy = pltpu.make_async_remote_copy(
            src_ref=piece(source, part),
            dst_ref=piece(ghosts.at[code(*offset)], part),
            send_sem=halo_send.at[len(halo)],
            recv_sem=halo_recv.at[2 * slot + (part or 0)],
            device_id=device(*to),
            device_id_type=MESH,
        )
        copy.start()
        halo.append(copy)

    def await_ghost(dx, dy, role, part=None):
        pltpu.make_async_remote_copy(
            src_ref=piece(dom, part),
            dst_ref=piece(ghost(dx, dy, role), part),
            send_sem=halo_send.at[0],
            recv_sem=halo_recv.at[2 * ghost_slot(dx, dy, role) + (part or 0)],
            device_id=device(0, 0, ON),
            device_id_type=MESH,
        ).wait_recv()

    def pass_x(source, e, dy, role, part):
        send_ghost(source, (e, 0, OWN), ghost_slot(-e, dy, role), (-e, dy, away(role)), part)

    def pass_y(source, e, dx, role, part):
        send_ghost(source, (0, e, OWN), ghost_slot(dx, -e, role), (dx, -e, away(role)), part)

    def pass_off(source, dx, dy, part):
        send_ghost(source, (0, 0, OFF), ghost_slot(dx, dy, OFF), (dx, dy, toward), part)

    def pass_on(source, dx, dy):
        send_ghost(source, (0, 0, ON), ghost_slot(dx, dy, ON), (dx, dy, -toward), None)

    for part in (0, 1):
        for e in (-1, 1):
            pass_y(dom, e, 0, OWN, part)
        for e in (-1, 1):
            pass_x(dom, e, 0, OWN, part)
        pass_off(dom, 0, 0, part)
    pass_on(dom, 0, 0)

    gathers = []

    def gather(source, target, to):
        number = len(gathers)
        copy = pltpu.make_async_remote_copy(
            src_ref=source,
            dst_ref=target,
            send_sem=gather_send.at[number],
            recv_sem=gather_recv.at[number],
            device_id=to,
            device_id_type=MESH,
        )
        copy.start()
        gathers.append(copy)
        return copy

    def spread_of_8(ref_of, at):
        for distance, moves in ((1, ((1, 2, 1, -1), (1, 0, 1, 1))), (3, ((0, 3, 3, -1), (1, 6, 2, 1)))):
            sent = [
                gather(ref_of(first, count), ref_of(target, count), at(sign * distance))
                for first, target, count, sign in moves
            ]
            yield
            for copy in sent:
                copy.wait_recv()

    def gather_steps():
        yield from spread_of_8(
            lambda first, count: group_z.at[pl.ds(8 * first, 8 * count)], lambda d: (me_x, me_y, at_z(d))
        )
        for a in range(3):
            group_xy[0, 1, 8 * a : 8 * a + 8, :] = group_z[pl.ds(a, 8, stride=8), :]
        yield from spread_of_8(
            lambda first, count: group_xy.at[0, pl.ds(first, count)], lambda d: (me_x, at_y(d), me_z)
        )
        sent = [
            gather(group_xy.at[0], group_xy.at[r], (at_x(-r), me_y, me_z)) for r in range(1, size_x)
        ]
        yield
        for copy in sent:
            copy.wait_recv()

    steps = gather_steps()

    def gather_step():
        next(steps, None)

    def features(b, carry):
        prepare_block(b, dom, feats, weights_rows)
        return carry

    def features_part(number):
        lax.fori_loop(4 * number, 4 * number + 4, features, 0, unroll=2)

    loads[1].wait()
    moments = lax.fori_loop(
        0, BLOCKS, lambda b, total: moment_block(b, dom, cells, total), jnp.zeros((16, 48), F32), unroll=4
    )
    group_z[8:16, :] = jnp.concatenate([moments[0:8], jnp.zeros((8, 80), F32)], axis=1)

    for part in (0, 1):
        await_ghost(0, 0, OFF, part)
        for e in (-1, 1):
            pass_x(ghost(0, 0, OFF), e, 0, OFF, part)
    await_ghost(0, 0, ON)
    gather_step()
    features_part(0)
    for part in (0, 1):
        for dx in (-1, 1):
            await_ghost(dx, 0, OWN, part)
            pass_y(ghost(dx, 0, OWN), -dx, dx, OWN, part)
    for dx in (-1, 1):
        pass_on(ghost(dx, 0, OWN), dx, 0)
    features_part(1)
    for part in (0, 1):
        for dy in (-1, 1):
            await_ghost(0, dy, OWN, part)
            pass_x(ghost(0, dy, OWN), dy, dy, OWN, part)
            pass_off(ghost(0, dy, OWN), 0, dy, part)
    for dy in (-1, 1):
        pass_on(ghost(0, dy, OWN), 0, dy)
    gather_step()
    features_part(2)
    for part in (0, 1):
        for dx in (-1, 1):
            await_ghost(dx, 0, OFF, part)
            pass_y(ghost(dx, 0, OFF), dx, dx, OFF, part)
    features_part(3)
    for part in (0, 1):
        for d in (-1, 1):
            await_ghost(d, d, OWN, part)
            pass_off(ghost(d, d, OWN), d, d, part)
    for d in (-1, 1):
        pass_on(ghost(d, d, OWN), d, d)
    features_part(4)
    for d in (-1, 1):
        for part in (0, 1):
            await_ghost(d, -d, OWN, part)
        pass_on(ghost(d, -d, OWN), d, -d)
    gather_step()
    for number in range(5, 8):
        features_part(number)

    ghosts[code(0, 0, 0)] = dom[...]
    rows = row_ids((8, WIDTH))
    for dx in SIDES:
        for dy in SIDES:
            for dz in SIDES:
                shifts[code(dx, dy, dz)] = jnp.where(
                    rows == 0,
                    dx - 0.5,
                    jnp.where(rows == 1, dy - 0.5, jnp.where(rows == 2, dz - 0.5, 0.0)),
                )
    loads[2].wait()
    node_tables(nodes, node_rows, node_hot)
    lines = [raw[3 + k] for k in range(3)]
    length = 0.5 * jnp.sqrt(lines[0] * lines[0] + lines[1] * lines[1] + lines[2] * lines[2])
    values[0] = head(length)
    values[1] = length - head(length)
    sums = node_sums(node_rows, node_hot, values, 1)
    node_len[...] = jnp.maximum(sums[0:32] + sums[32:64], DRAG_FLOOR)
    for load in loads[3:]:
        load.wait()

    for part in (0, 1):
        for dy in (-1, 1):
            await_ghost(0, dy, OFF, part)
        for d in (-1, 1):
            await_ghost(d, -d, OFF, part)
            await_ghost(d, d, OFF, part)
    for dx in SIDES:
        for dy in SIDES:
            if (dx, dy) != (0, 0):
                await_ghost(dx, dy, ON)

    def pair_part(first, last):
        def body(group, carry):
            pair_group(
                group, blocks, codes, dom, ghosts, shifts, feats, weights_rows, own_out, peer_out, UNROLL
            )
            return carry

        lax.fori_loop(first // UNROLL, last // UNROLL, body, 0)

    gather_step()
    pair_part(0, 64)
    gather_step()
    pair_part(64, SLOTS)

    live = count[0]
    table = slot_table(peer_out, live)
    code_row = code_ids[...]
    side = (code_row * 43) >> 7
    away_z = code_row - 3 * side - 1
    role_row = jnp.where(away_z == 0, OWN, jnp.where(away_z == toward, ON, OFF))
    targets = (role_row * 9 + side) * BLOCKS + block_ids[1:2, :]
    reacts = []

    def send_react(source, target_ref, target, number):
        copy = pltpu.make_async_remote_copy(
            src_ref=source,
            dst_ref=target_ref,
            send_sem=react_send.at[number],
            recv_sem=react_recv.at[number],
            device_id=target,
            device_id_type=MESH,
        )
        copy.start()
        reacts.append(copy)

    react[ON] = dot(slot_hot(targets, 288, 288), table)
    send_react(react.at[ON], from_on, device(0, 0, ON), 0)
    react[OFF] = dot(slot_hot(targets, 576, 288), table)
    for dx in SIDES:
        for dy in SIDES:
            d = ghost_slot(dx, dy, 0)
            send_react(
                react.at[OFF, pl.ds(32 * d, 32)], from_off.at[pl.ds(32 * d, 32)], device(dx, dy, OFF), 1 + d
            )
    react[OWN] = dot(slot_hot(targets, 0, 288), table)
    reacts[0].wait_recv()
    react[OWN] = react[OWN] + from_on[...]
    sent = [(dx, dy) for dx in SIDES for dy in SIDES if (dx, dy) != (0, 0)]
    for number, (dx, dy) in enumerate(sent):
        d = ghost_slot(dx, dy, 0)
        send_react(
            react.at[OWN, pl.ds(32 * d, 32)], from_layer.at[number], device(dx, dy, OWN), 10 + number
        )

    near = dot(slot_hot(block_ids[0:1, :], 0, BLOCKS), slot_table(own_out, live))
    near = near + react[OWN, pl.ds(128, 32), :]

    for _ in steps:
        pass
    sides = []
    for a in range(3):
        held = group_xy[:, :, 8 * a : 8 * a + 8, :].reshape(256, WIDTH)
        first = held.astype(BF16)
        second = (held - first.astype(F32)).astype(BF16)
        sides.append(jnp.concatenate([first, second, first], axis=0))
    spread = dot(far_table[...], jnp.concatenate(sides, axis=1))
    source = lax.broadcasted_iota(jnp.int32, (256, 384), 0) >> 4
    lane = lax.broadcasted_iota(jnp.int32, (256, 384), 1) & 15
    spread = jnp.where(source == lane, spread, 0.0)
    folded = spread[0:16]
    for k in range(1, 16):
        folded = folded + spread[16 * k : 16 * k + 16]
    folded = jnp.concatenate([folded, jnp.zeros((112, 384), F32)], axis=0)
    first = folded.astype(BF16)
    second = (folded - first.astype(F32)).astype(BF16)
    field = dot_nt(fold[...], jnp.concatenate([first, second], axis=1))
    cell = cells[...]
    hits = [cell == m for m in range(CELL_DEV)]
    per_seg = []
    for m in range(9):
        held = jnp.zeros((BLOCKS, WIDTH), F32)
        for k in range(CELL_DEV):
            held = jnp.where(hits[k], field[m : m + 1, k : k + 1], held)
        per_seg.append(held)
    burgers = [raw[6], raw[7], raw[8]]
    lines = [raw[3 + k] for k in range(3)]
    pulled = [sum(per_seg[3 * a + k] * burgers[k] for k in range(3)) for a in range(3)]
    force = [
        pulled[1] * lines[2] - pulled[2] * lines[1],
        pulled[2] * lines[0] - pulled[0] * lines[2],
        pulled[0] * lines[1] - pulled[1] * lines[0],
    ]

    for copy in reacts[1:]:
        copy.wait_recv()
    for number in range(8):
        near = near + from_layer[number]
    for d in range(9):
        near = near + from_off[pl.ds(32 * d, 32), :]
    for c in range(3):
        half = 0.5 * (force[c] + near[:, 128 * c : 128 * c + 128])
        values[c] = head(half)
        values[3 + c] = half - head(half)
    sums = node_sums(node_rows, node_hot, values, 3)
    for c in range(3):
        out[c] = (sums[32 * c : 32 * c + 32] + sums[96 + 32 * c : 128 + 32 * c]) / node_len[...]

    for copy in halo + gathers + reacts:
        copy.wait_send()


def shards(seg_state, seg_cells, seg_nodes, pair_blocks, pair_offsets, pair_count):
    far_table, fold = far_tables()
    anywhere = pl.BlockSpec(memory_space=pltpu.HBM)
    out = pl.pallas_call(
        kernel,
        out_shape=jax.ShapeDtypeStruct((3, BLOCKS, WIDTH), F32),
        in_specs=[anywhere] * 5 + [pl.BlockSpec(memory_space=pltpu.SMEM)] + [anywhere] * 2,
        out_specs=pl.BlockSpec(memory_space=pltpu.VMEM),
        scratch_shapes=[
            pltpu.VMEM((9, BLOCKS, WIDTH), F32),
            pltpu.VMEM((BLOCKS, WIDTH), jnp.int32),
            pltpu.VMEM((2, BLOCKS * WIDTH), jnp.int32),
            pltpu.VMEM((2, SLOTS), jnp.int32),
            pltpu.VMEM((1, SLOTS), jnp.int32),
            pltpu.SMEM((2, SLOTS), jnp.int32),
            pltpu.SMEM((1, SLOTS), jnp.int32),
            pltpu.VMEM(far_table.shape, BF16),
            pltpu.VMEM(fold.shape, BF16),
            pltpu.VMEM((TILES, 8, WIDTH), F32),
            pltpu.VMEM((27, TILES, 8, WIDTH), F32),
            pltpu.VMEM((27, 8, WIDTH), F32),
            pltpu.VMEM((BLOCKS, 256, WIDTH), BF16),
            pltpu.VMEM((BLOCKS, 16, 256), BF16),
            pltpu.VMEM((SLOTS, 8, WIDTH), F32),
            pltpu.VMEM((SLOTS, 8, WIDTH), F32),
            pltpu.VMEM((3, 288, 384), F32),
            pltpu.VMEM((288, 384), F32),
            pltpu.VMEM((288, 384), F32),
            pltpu.VMEM((8, 32, 384), F32),
            pltpu.VMEM((2, BLOCKS, WIDTH), jnp.int32),
            pltpu.VMEM((BLOCKS, 256, WIDTH), BF16),
            pltpu.VMEM((32, WIDTH), F32),
            pltpu.VMEM((6, BLOCKS, WIDTH), F32),
            pltpu.VMEM((64, WIDTH), F32),
            pltpu.VMEM((4, 8, 24, WIDTH), F32),
            pltpu.SemaphoreType.DMA((9,)),
            pltpu.SemaphoreType.DMA((43,)),
            pltpu.SemaphoreType.DMA((54,)),
            pltpu.SemaphoreType.DMA((18,)),
            pltpu.SemaphoreType.DMA((18,)),
            pltpu.SemaphoreType.DMA((11,)),
            pltpu.SemaphoreType.DMA((11,)),
        ],
        compiler_params=pltpu.CompilerParams(
            collective_id=0, has_side_effects=True, vmem_limit_bytes=62 * 1024 * 1024
        ),
    )(
        jnp.transpose(seg_state[0, 0, 0], (1, 0, 2)),
        seg_cells[0, 0, 0],
        seg_nodes[0, 0, 0],
        pair_blocks[0, 0, 0],
        pair_offsets[0, 0],
        pair_count.reshape(1),
        jnp.asarray(far_table),
        jnp.asarray(fold),
    )
    return out.reshape(1, 1, 1, 3, BLOCKS * WIDTH)


def solution(mesh):
    placed = (
        P("gx", "gy", "gz", None, None, None),
        P("gx", "gy", "gz", None, None),
        P("gx", "gy", "gz", None, None),
        P("gx", "gy", "gz", None, None),
        P("gx", "gy", "gz", None),
        P("gx", "gy", "gz"),
    )
    return jax.shard_map(
        shards,
        mesh=mesh,
        in_specs=placed,
        out_specs=P("gx", "gy", "gz", None, None),
        check_vma=False,
    )
```

```python
import jax
import jax.numpy as jnp
import numpy as np
from jax import lax
from jax.experimental import pallas as pl
from jax.experimental.pallas import tpu as pltpu
from jax.sharding import PartitionSpec as P

CELLS = 16
PAIR_STRENGTH = 0.1
CORE_SQUARED = 0.2
FAR_STRENGTH = 0.008
DRAG_FLOOR = 0.5

BLOCKS = 32
WIDTH = 128
SLOTS = 128
TILES = 36
CELL_DEV = 16
UNROLL = 64
LAG1, LAG2, LAG3 = (3, 4, 5)
TOGETHER = 32
SIDES = (-1, 0, 1)
F32 = jnp.float32
BF16 = jnp.bfloat16
MESH = pl.DeviceIdType.MESH
NT = (((1,), (1,)), ((), ()))
PAIR_SCALE = float(PAIR_STRENGTH * (1.0 / CORE_SQUARED) ** 1.5)
OWN, ON, OFF = 0, 1, 2


def ghost_slot(dx, dy, role):
    return role * 9 + (dx + 1) * 3 + dy + 1


def dot(first, second):
    return jnp.dot(first, second, preferred_element_type=F32)


def dot_nt(first, second):
    return lax.dot_general(first, second, NT, preferred_element_type=F32)


def head(value):
    return value.astype(BF16).astype(F32)


def pair16(low, high):
    return jnp.concatenate([low, high], axis=0).astype(BF16)


def row_ids(shape):
    return lax.broadcasted_iota(jnp.int32, shape, 0)


def block_rows(tile, last, rows):
    turned = pltpu.roll(tile, 5, 0)
    line = jnp.where(rows < 3, turned, tile)
    burgers = jnp.where(rows < 2, pltpu.roll(tile, 2, 0), turned)
    burgers = jnp.where((rows == 2) | (rows == 5), last, burgers)
    return line, burgers


def outer_rows(first, second, rows):
    low = jnp.where(rows < 3, first[0:1], first[1:2]) * second
    low = jnp.where(rows < 6, low, 0.0)
    high = jnp.where(rows < 3, first[2:3] * second, 0.0)
    return low, high


def dist_rows(place, norm_row, one_row, rows):
    return jnp.where(rows < 3, place, jnp.where(rows == 3, norm_row, jnp.where(rows == 4, one_row, 0.0)))


def prepare_block(i, dom, feats, weights_rows):
    rows = row_ids((8, WIDTH))
    tile = dom[i]
    last = dom[32 + (i >> 3), pl.ds(i & 7, 1), :]
    line, burgers = block_rows(tile, last, rows)
    place = jnp.where(rows < 3, tile - 0.5, 0.0)
    norm = jnp.sum(place * place, axis=0, keepdims=True)
    scale = 1.0 / CORE_SQUARED
    same = jnp.concatenate(outer_rows(line, burgers, rows), axis=0)
    same_1 = head(same)
    crossed = jnp.concatenate(outer_rows(burgers, line, rows), axis=0)
    crossed_1 = head(crossed)
    dist = dist_rows(-2.0 * scale * place, scale, scale * norm + 1.0, rows)
    first = head(dist)
    second = head(dist - first)
    third = head(dist - first - second)
    gap = jnp.zeros((16, WIDTH), F32)
    stack = jnp.concatenate([same_1, same_1, same - same_1, gap, first, first, first, second, second, third, gap], axis=0)
    feats[i, 0:WIDTH] = jnp.transpose(stack).astype(BF16)
    stack = jnp.concatenate([crossed_1, crossed_1, crossed - crossed_1, jnp.zeros((80, WIDTH), F32)], axis=0)
    feats[i, WIDTH : 2 * WIDTH] = jnp.transpose(stack).astype(BF16)
    place_first = head(place)
    ones = jnp.where(rows == 3, 1.0, 0.0)
    held = pair16(place_first + ones, place - place_first)
    weights_rows[i] = jnp.concatenate([held, held], axis=1)


def pair_group(group, blocks, codes, dom, ghosts, shifts, feats, weights_rows, own_out, peer_out, unroll):
    rows = row_ids((8, WIDTH))
    centre = jnp.where(rows < 3, 0.5, 0.0)
    def load(u):
        slot = group * unroll + u
        i = blocks[0, slot]
        g = codes[0, slot]
        j = blocks[1, slot]
        tile = ghosts[g, j]
        last = ghosts[g, 32 + (j >> 3), pl.ds(j & 7, 1), :]
        line, burgers = block_rows(tile, last, rows)
        place = jnp.where(rows < 3, tile + shifts[g], 0.0)
        norm = jnp.sum(place * place, axis=0, keepdims=True)
        product = jnp.concatenate(outer_rows(line, burgers, rows), axis=0)
        product_1 = product.astype(BF16)
        product_2 = (product - product_1.astype(F32)).astype(BF16)
        products = jnp.concatenate([product_1, product_2, product_1], axis=0)
        dist = dist_rows(place, norm, 1.0, rows)
        first = head(dist)
        rest = dist - first
        second = head(rest)
        dists = jnp.concatenate(
            [
                jnp.zeros((64, WIDTH), BF16),
                pair16(first, second),
                pair16(rest - second, first),
                pair16(second, first),
                jnp.zeros((16, WIDTH), BF16),
            ],
            axis=0,
        )
        held = pair16(first, second)
        return slot, i, place, products, dists, held

    def multiply(slot, i, place, products, dists, held):
        return dot(feats[i][:, :48], products), dot(feats[i, 0:WIDTH], dists)

    def strength_of(both, dist):
        inv = lax.rsqrt(dist)
        inv_sq = inv * inv
        strength = (inv_sq * inv) * (both[0:128] + both[128:256] * inv_sq)
        high = strength.astype(BF16)
        return high, (strength - high.astype(F32)).astype(BF16)

    def reduce(slot, i, place, products, dists, held, high, low):
        peer = dot(weights_rows[i], jnp.concatenate([high, low], axis=0))
        own = dot_nt(jnp.concatenate([held, held], axis=1), jnp.concatenate([high, low], axis=1))
        peer = peer[0:8] + peer[8:16]
        own = own[0:8] + own[8:16]
        home = dom[i] - centre
        own_out[slot] = home * own[4:5] - own
        peer_out[slot] = place * peer[3:4] - peer

    loaded, outs, strengths = {}, {}, {}
    for turn in range(unroll + LAG1 + LAG2 + LAG3):
        if turn < unroll:
            loaded[turn] = load(turn)
        u = turn - LAG1
        if 0 <= u < unroll:
            outs[u] = multiply(*loaded[u])
        u -= LAG2
        if 0 <= u < unroll:
            strengths[u] = strength_of(*outs.pop(u))
        u -= LAG3
        if 0 <= u < unroll:
            reduce(*loaded.pop(u), *strengths.pop(u))


def slot_table(slot_out, live):
    keep = row_ids((SLOTS, WIDTH)) < live
    parts = [
        jnp.where(keep, PAIR_SCALE * slot_out[:, c, :], 0.0) for c in range(3)
    ]
    table = jnp.concatenate(parts, axis=1)
    first = table.astype(BF16)
    return jnp.concatenate([first, (table - first.astype(F32)).astype(BF16)], axis=0)


def slot_hot(targets, base, count):
    ids = row_ids((count, SLOTS)) + base
    hot = jnp.where(ids == targets, 1.0, 0.0).astype(BF16)
    return jnp.concatenate([hot, hot], axis=1)


def moment_block(b, dom, cells, total):
    rows = row_ids((8, WIDTH))
    tile = dom[b]
    last = dom[32 + (b >> 3), pl.ds(b & 7, 1), :]
    line, burgers = block_rows(tile, last, rows)
    hot = row_ids((CELL_DEV, WIDTH)) == cells[pl.ds(b, 1), :]
    line_1 = head(line)
    line_2 = line - line_1
    burgers = jnp.where(rows < 3, burgers, 0.0)
    burgers_1 = head(burgers)
    burgers_2 = burgers - burgers_1
    zero = jnp.zeros((CELL_DEV, WIDTH), F32)
    spread = [
        jnp.concatenate([jnp.where(hot, part[k : k + 1], zero) for k in range(3)], axis=0).astype(BF16)
        for part in (line_1, line_2)
    ]
    pad = jnp.zeros((8, WIDTH), F32)
    left = jnp.concatenate([pair16(burgers_1, pad), pair16(burgers_1, pad), pair16(burgers_2, pad)], axis=1)
    right = jnp.concatenate([spread[0], spread[1], spread[0]], axis=1)
    return total + dot_nt(left, right)


def node_tables(nodes, node_rows, node_hot):
    def copy_row(b, carry):
        for e in range(2):
            node_rows[e, pl.ds(b, 1), :] = nodes[e : e + 1, pl.ds(pl.multiple_of(b * WIDTH, WIDTH), WIDTH)]
        return carry

    lax.fori_loop(0, BLOCKS, copy_row, 0, unroll=4)
    lanes = lax.broadcasted_iota(jnp.int32, (WIDTH, WIDTH), 1).astype(F32)
    for e in range(2):
        lows = (node_rows[e] & 127).astype(F32)
        turned = jnp.transpose(jnp.concatenate([lows, jnp.zeros((96, WIDTH), F32)], axis=0))
        for b in range(BLOCKS):
            node_hot[b, e * WIDTH : (e + 1) * WIDTH, :] = jnp.where(turned[:, b : b + 1] == lanes, 1.0, 0.0).astype(BF16)


def node_sums(node_rows, node_hot, values, count):
    together = TOGETHER

    def body(turn, total):
        parts, hots = [], []
        for u in range(together):
            b = turn * together + u
            for e in range(2):
                hit = row_ids((32, WIDTH)) == node_rows[e, pl.ds(b, 1), :] >> 7
                rows = [jnp.where(hit, values[c, pl.ds(b, 1), :], 0.0) for c in range(2 * count)]
                parts.append(jnp.concatenate(rows, axis=0).astype(BF16))
            hots.append(node_hot[b])
        return total + dot(jnp.concatenate(parts, axis=1), jnp.concatenate(hots, axis=0))

    return lax.fori_loop(0, BLOCKS // together, body, jnp.zeros((64 * count, WIDTH), F32))


def far_tables():
    index = np.arange(CELL_DEV)
    inner = np.stack([index // 4, index // 2 % 2, index % 2])
    rel = np.arange(256)
    away = np.stack([rel // 64 * 4, (rel // 8 % 8 - 1) * 2, (rel % 8 - 1) * 2])
    delta = away[:, None, None, :] + inner[:, :, None, None] - inner[:, None, :, None]
    delta = (delta + 8) % 16 - 8
    dist = np.sqrt(np.maximum((delta.astype(np.float64) ** 2).sum(0), 1.0))
    far = np.where(np.abs(delta).max(0) > 1, FAR_STRENGTH / dist, 0.0).astype(np.float32)
    lanes = np.arange(384)
    part = lanes % 128
    fold = np.zeros((16, 384), np.float32)
    for lane in lanes[part < 48]:
        fold[3 * (lane // 128) + part[lane] // 16, lane] = 1.0
    return far.reshape(256, 256), fold


def kernel(
    state_in, cells_in, nodes_in, blocks_in, codes_in, count, far_in, fold_in, out,
    raw, cells, nodes, block_ids, code_ids, blocks, codes, far_table, fold,
    dom, ghosts, shifts, feats, weights_rows, own_out, peer_out, react, from_on, from_off, from_layer,
    node_rows, node_hot, node_len, values, group_z, group_xy,
    load_sem, halo_send, halo_recv, react_send, react_recv, gather_send, gather_recv,
):
    size_x, size_y, size_z = 4, 8, 8
    me_x = lax.axis_index("gx")
    me_y = lax.axis_index("gy")
    me_z = lax.axis_index("gz")
    toward = 1 - 2 * lax.rem(me_z, 2)

    loads = [
        pltpu.make_async_copy(source, target, load_sem.at[number])
        for number, (source, target) in enumerate(
            [
                (state_in, raw), (cells_in, cells), (nodes_in, nodes), (blocks_in, blocks), (codes_in, codes),
                (blocks_in, block_ids), (codes_in, code_ids), (far_in, far_table), (fold_in, fold),
            ]
        )
    ]
    for load in loads:
        load.start()

    def at_x(d):
        return lax.rem(me_x + d + size_x, size_x)

    def at_y(d):
        return lax.rem(me_y + d + size_y, size_y)

    def at_z(d):
        return lax.rem(me_z + d + size_z, size_z)

    def away(role):
        return 0 if role == OWN else (toward if role == ON else -toward)

    def device(dx, dy, role):
        return (at_x(dx), at_y(dy), at_z(away(role)))

    def code(dx, dy, dz):
        return (dx + 1) * 9 + (dy + 1) * 3 + dz + 1

    peers = [
        device(-1, 0, OWN), device(1, 0, OWN), device(0, -1, OWN), device(0, 1, OWN), device(0, 0, OFF), device(0, 0, ON)
    ]
    barrier = pltpu.get_barrier_semaphore()
    for peer in peers:
        pl.semaphore_signal(barrier, inc=1, device_id=peer, device_id_type=MESH)
    loads[0].wait()
    for k in range(8):
        dom[0:BLOCKS, k, :] = raw[k]
    dom[BLOCKS:TILES] = raw[8].reshape(4, 8, WIDTH)
    pl.semaphore_wait(barrier, len(peers))

    halo = []
    half = TILES // 2

    def piece(ref, part):
        return ref if part is None else ref.at[pl.ds(part * half, half)]

    def ghost(dx, dy, role):
        return ghosts.at[code(dx, dy, away(role))]

    def send_ghost(source, to, slot, offset, part):
        copy = pltpu.make_async_remote_copy(
            src_ref=piece(source, part),
            dst_ref=piece(ghosts.at[code(*offset)], part),
            send_sem=halo_send.at[len(halo)],
            recv_sem=halo_recv.at[2 * slot + (part or 0)],
            device_id=device(*to),
            device_id_type=MESH,
        )
        copy.start()
        halo.append(copy)

    def await_ghost(dx, dy, role, part=None):
        pltpu.make_async_remote_copy(
            src_ref=piece(dom, part),
            dst_ref=piece(ghost(dx, dy, role), part),
            send_sem=halo_send.at[0],
            recv_sem=halo_recv.at[2 * ghost_slot(dx, dy, role) + (part or 0)],
            device_id=device(0, 0, ON),
            device_id_type=MESH,
        ).wait_recv()

    def pass_x(source, e, dy, role, part):
        send_ghost(source, (e, 0, OWN), ghost_slot(-e, dy, role), (-e, dy, away(role)), part)

    def pass_y(source, e, dx, role, part):
        send_ghost(source, (0, e, OWN), ghost_slot(dx, -e, role), (dx, -e, away(role)), part)

    def pass_off(source, dx, dy, part):
        send_ghost(source, (0, 0, OFF), ghost_slot(dx, dy, OFF), (dx, dy, toward), part)

    def pass_on(source, dx, dy):
        send_ghost(source, (0, 0, ON), ghost_slot(dx, dy, ON), (dx, dy, -toward), None)

    for part in (0, 1):
        for e in (-1, 1):
            pass_y(dom, e, 0, OWN, part)
        for e in (-1, 1):
            pass_x(dom, e, 0, OWN, part)
        pass_off(dom, 0, 0, part)
    pass_on(dom, 0, 0)

    gathers = []

    def gather(source, target, to):
        number = len(gathers)
        copy = pltpu.make_async_remote_copy(
            src_ref=source,
            dst_ref=target,
            send_sem=gather_send.at[number],
            recv_sem=gather_recv.at[number],
            device_id=to,
            device_id_type=MESH,
        )
        copy.start()
        gathers.append(copy)
        return copy

    def spread_of_8(ref_of, at):
        for distance, moves in ((1, ((1, 2, 1, -1), (1, 0, 1, 1))), (3, ((0, 3, 3, -1), (1, 6, 2, 1)))):
            sent = [
                gather(ref_of(first, count), ref_of(target, count), at(sign * distance))
                for first, target, count, sign in moves
            ]
            yield
            for copy in sent:
                copy.wait_recv()

    def gather_steps():
        yield from spread_of_8(
            lambda first, count: group_z.at[pl.ds(8 * first, 8 * count)], lambda d: (me_x, me_y, at_z(d))
        )
        for a in range(3):
            group_xy[0, 1, 8 * a : 8 * a + 8, :] = group_z[pl.ds(a, 8, stride=8), :]
        yield from spread_of_8(
            lambda first, count: group_xy.at[0, pl.ds(first, count)], lambda d: (me_x, at_y(d), me_z)
        )
        sent = [
            gather(group_xy.at[0], group_xy.at[r], (at_x(-r), me_y, me_z)) for r in range(1, size_x)
        ]
        yield
        for copy in sent:
            copy.wait_recv()

    steps = gather_steps()

    def gather_step():
        next(steps, None)

    def features(b, carry):
        prepare_block(b, dom, feats, weights_rows)
        return carry

    def features_part(number):
        lax.fori_loop(4 * number, 4 * number + 4, features, 0, unroll=2)

    loads[1].wait()
    moments = lax.fori_loop(
        0, BLOCKS, lambda b, total: moment_block(b, dom, cells, total), jnp.zeros((16, 48), F32), unroll=4
    )
    group_z[8:16, :] = jnp.concatenate([moments[0:8], jnp.zeros((8, 80), F32)], axis=1)

    for part in (0, 1):
        await_ghost(0, 0, OFF, part)
        for e in (-1, 1):
            pass_x(ghost(0, 0, OFF), e, 0, OFF, part)
    await_ghost(0, 0, ON)
    gather_step()
    features_part(0)
    for part in (0, 1):
        for dx in (-1, 1):
            await_ghost(dx, 0, OWN, part)
            pass_y(ghost(dx, 0, OWN), -dx, dx, OWN, part)
    for dx in (-1, 1):
        pass_on(ghost(dx, 0, OWN), dx, 0)
    features_part(1)
    for part in (0, 1):
        for dy in (-1, 1):
            await_ghost(0, dy, OWN, part)
            pass_x(ghost(0, dy, OWN), dy, dy, OWN, part)
            pass_off(ghost(0, dy, OWN), 0, dy, part)
    for dy in (-1, 1):
        pass_on(ghost(0, dy, OWN), 0, dy)
    gather_step()
    features_part(2)
    for part in (0, 1):
        for dx in (-1, 1):
            await_ghost(dx, 0, OFF, part)
            pass_y(ghost(dx, 0, OFF), dx, dx, OFF, part)
    features_part(3)
    for part in (0, 1):
        for d in (-1, 1):
            await_ghost(d, d, OWN, part)
            pass_off(ghost(d, d, OWN), d, d, part)
    for d in (-1, 1):
        pass_on(ghost(d, d, OWN), d, d)
    gather_step()
    features_part(4)
    for d in (-1, 1):
        for part in (0, 1):
            await_ghost(d, -d, OWN, part)
        pass_on(ghost(d, -d, OWN), d, -d)
    for number in range(5, 8):
        features_part(number)

    ghosts[code(0, 0, 0)] = dom[...]
    rows = row_ids((8, WIDTH))
    for dx in SIDES:
        for dy in SIDES:
            for dz in SIDES:
                shifts[code(dx, dy, dz)] = jnp.where(
                    rows == 0,
                    dx - 0.5,
                    jnp.where(rows == 1, dy - 0.5, jnp.where(rows == 2, dz - 0.5, 0.0)),
                )
    loads[2].wait()
    node_tables(nodes, node_rows, node_hot)
    lines = [raw[3 + k] for k in range(3)]
    length = 0.5 * jnp.sqrt(lines[0] * lines[0] + lines[1] * lines[1] + lines[2] * lines[2])
    values[0] = head(length)
    values[1] = length - head(length)
    sums = node_sums(node_rows, node_hot, values, 1)
    node_len[...] = jnp.maximum(sums[0:32] + sums[32:64], DRAG_FLOOR)
    for load in loads[3:]:
        load.wait()

    for part in (0, 1):
        for dy in (-1, 1):
            await_ghost(0, dy, OFF, part)
        for d in (-1, 1):
            await_ghost(d, -d, OFF, part)
            await_ghost(d, d, OFF, part)
    for dx in SIDES:
        for dy in SIDES:
            if (dx, dy) != (0, 0):
                await_ghost(dx, dy, ON)

    def pair_part(first, last):
        def body(group, carry):
            pair_group(
                group, blocks, codes, dom, ghosts, shifts, feats, weights_rows, own_out, peer_out, UNROLL
            )
            return carry

        lax.fori_loop(first // UNROLL, last // UNROLL, body, 0)

    gather_step()
    pair_part(0, 64)
    gather_step()
    pair_part(64, SLOTS)

    live = count[0]
    table = slot_table(peer_out, live)
    code_row = code_ids[...]
    side = (code_row * 43) >> 7
    away_z = code_row - 3 * side - 1
    role_row = jnp.where(away_z == 0, OWN, jnp.where(away_z == toward, ON, OFF))
    targets = (role_row * 9 + side) * BLOCKS + block_ids[1:2, :]
    reacts = []

    def send_react(source, target_ref, target, number):
        copy = pltpu.make_async_remote_copy(
            src_ref=source,
            dst_ref=target_ref,
            send_sem=react_send.at[number],
            recv_sem=react_recv.at[number],
            device_id=target,
            device_id_type=MESH,
        )
        copy.start()
        reacts.append(copy)

    react[ON] = dot(slot_hot(targets, 288, 288), table)
    send_react(react.at[ON], from_on, device(0, 0, ON), 0)
    react[OFF] = dot(slot_hot(targets, 576, 288), table)
    for dx in SIDES:
        for dy in SIDES:
            d = ghost_slot(dx, dy, 0)
            send_react(
                react.at[OFF, pl.ds(32 * d, 32)], from_off.at[pl.ds(32 * d, 32)], device(dx, dy, OFF), 1 + d
            )
    react[OWN] = dot(slot_hot(targets, 0, 288), table)
    reacts[0].wait_recv()
    react[OWN] = react[OWN] + from_on[...]
    sent = [(dx, dy) for dx in SIDES for dy in SIDES if (dx, dy) != (0, 0)]
    for number, (dx, dy) in enumerate(sent):
        d = ghost_slot(dx, dy, 0)
        send_react(
            react.at[OWN, pl.ds(32 * d, 32)], from_layer.at[number], device(dx, dy, OWN), 10 + number
        )

    near = dot(slot_hot(block_ids[0:1, :], 0, BLOCKS), slot_table(own_out, live))
    near = near + react[OWN, pl.ds(128, 32), :]

    for _ in steps:
        pass
    sides = []
    for a in range(3):
        held = group_xy[:, :, 8 * a : 8 * a + 8, :].reshape(256, WIDTH)
        first = held.astype(BF16)
        second = (held - first.astype(F32)).astype(BF16)
        sides.append(jnp.concatenate([first, second, first], axis=0))
    far = far_table[...]
    first = far.astype(BF16)
    second = (far - first.astype(F32)).astype(BF16)
    spread = dot(jnp.concatenate([first, first, second], axis=1), jnp.concatenate(sides, axis=1))
    source = lax.broadcasted_iota(jnp.int32, (256, 384), 0) >> 4
    lane = lax.broadcasted_iota(jnp.int32, (256, 384), 1) & 15
    spread = jnp.where(source == lane, spread, 0.0)
    folded = spread[0:16]
    for k in range(1, 16):
        folded = folded + spread[16 * k : 16 * k + 16]
    folded = jnp.concatenate([folded, jnp.zeros((112, 384), F32)], axis=0)
    first = folded.astype(BF16)
    second = (folded - first.astype(F32)).astype(BF16)
    folds = fold[...].astype(BF16)
    field = dot_nt(jnp.concatenate([folds, folds], axis=1), jnp.concatenate([first, second], axis=1))
    cell = cells[...]
    hits = [cell == m for m in range(CELL_DEV)]
    per_seg = []
    for m in range(9):
        held = jnp.zeros((BLOCKS, WIDTH), F32)
        for k in range(CELL_DEV):
            held = jnp.where(hits[k], field[m : m + 1, k : k + 1], held)
        per_seg.append(held)
    burgers = [raw[6], raw[7], raw[8]]
    lines = [raw[3 + k] for k in range(3)]
    pulled = [sum(per_seg[3 * a + k] * burgers[k] for k in range(3)) for a in range(3)]
    force = [
        pulled[1] * lines[2] - pulled[2] * lines[1],
        pulled[2] * lines[0] - pulled[0] * lines[2],
        pulled[0] * lines[1] - pulled[1] * lines[0],
    ]

    for copy in reacts[1:]:
        copy.wait_recv()
    for number in range(8):
        near = near + from_layer[number]
    for d in range(9):
        near = near + from_off[pl.ds(32 * d, 32), :]
    for c in range(3):
        half = 0.5 * (force[c] + near[:, 128 * c : 128 * c + 128])
        values[c] = head(half)
        values[3 + c] = half - head(half)
    sums = node_sums(node_rows, node_hot, values, 3)
    for c in range(3):
        out[c] = (sums[32 * c : 32 * c + 32] + sums[96 + 32 * c : 128 + 32 * c]) / node_len[...]

    for copy in halo + gathers + reacts:
        copy.wait_send()


def shards(seg_state, seg_cells, seg_nodes, pair_blocks, pair_offsets, pair_count):
    far_table, fold = far_tables()
    anywhere = pl.BlockSpec(memory_space=pltpu.HBM)
    out = pl.pallas_call(
        kernel,
        out_shape=jax.ShapeDtypeStruct((3, BLOCKS, WIDTH), F32),
        in_specs=[anywhere] * 5 + [pl.BlockSpec(memory_space=pltpu.SMEM)] + [anywhere] * 2,
        out_specs=pl.BlockSpec(memory_space=pltpu.VMEM),
        scratch_shapes=[
            pltpu.VMEM((9, BLOCKS, WIDTH), F32),
            pltpu.VMEM((BLOCKS, WIDTH), jnp.int32),
            pltpu.VMEM((2, BLOCKS * WIDTH), jnp.int32),
            pltpu.VMEM((2, SLOTS), jnp.int32),
            pltpu.VMEM((1, SLOTS), jnp.int32),
            pltpu.SMEM((2, SLOTS), jnp.int32),
            pltpu.SMEM((1, SLOTS), jnp.int32),
            pltpu.VMEM(far_table.shape, F32),
            pltpu.VMEM(fold.shape, F32),
            pltpu.VMEM((TILES, 8, WIDTH), F32),
            pltpu.VMEM((27, TILES, 8, WIDTH), F32),
            pltpu.VMEM((27, 8, WIDTH), F32),
            pltpu.VMEM((BLOCKS, 256, WIDTH), BF16),
            pltpu.VMEM((BLOCKS, 16, 256), BF16),
            pltpu.VMEM((SLOTS, 8, WIDTH), F32),
            pltpu.VMEM((SLOTS, 8, WIDTH), F32),
            pltpu.VMEM((3, 288, 384), F32),
            pltpu.VMEM((288, 384), F32),
            pltpu.VMEM((288, 384), F32),
            pltpu.VMEM((8, 32, 384), F32),
            pltpu.VMEM((2, BLOCKS, WIDTH), jnp.int32),
            pltpu.VMEM((BLOCKS, 256, WIDTH), BF16),
            pltpu.VMEM((32, WIDTH), F32),
            pltpu.VMEM((6, BLOCKS, WIDTH), F32),
            pltpu.VMEM((64, WIDTH), F32),
            pltpu.VMEM((4, 8, 24, WIDTH), F32),
            pltpu.SemaphoreType.DMA((9,)),
            pltpu.SemaphoreType.DMA((43,)),
            pltpu.SemaphoreType.DMA((54,)),
            pltpu.SemaphoreType.DMA((18,)),
            pltpu.SemaphoreType.DMA((18,)),
            pltpu.SemaphoreType.DMA((11,)),
            pltpu.SemaphoreType.DMA((11,)),
        ],
        compiler_params=pltpu.CompilerParams(
            collective_id=0, has_side_effects=True, vmem_limit_bytes=62 * 1024 * 1024
        ),
    )(
        jnp.transpose(seg_state[0, 0, 0], (1, 0, 2)),
        seg_cells[0, 0, 0],
        seg_nodes[0, 0, 0],
        pair_blocks[0, 0, 0],
        pair_offsets[0, 0],
        pair_count.reshape(1),
        jnp.asarray(far_table),
        jnp.asarray(fold),
    )
    return out.reshape(1, 1, 1, 3, BLOCKS * WIDTH)


def solution(mesh):
    placed = (
        P("gx", "gy", "gz", None, None, None),
        P("gx", "gy", "gz", None, None),
        P("gx", "gy", "gz", None, None),
        P("gx", "gy", "gz", None, None),
        P("gx", "gy", "gz", None),
        P("gx", "gy", "gz"),
    )
    return jax.shard_map(
        shards,
        mesh=mesh,
        in_specs=placed,
        out_specs=P("gx", "gy", "gz", None, None),
        check_vma=False,
    )
```

```python
import jax
import jax.numpy as jnp
import numpy as np
from jax import lax
from jax.experimental import pallas as pl
from jax.experimental.pallas import tpu as pltpu
from jax.sharding import PartitionSpec as P

CELLS = 16
PAIR_STRENGTH = 0.1
CORE_SQUARED = 0.2
FAR_STRENGTH = 0.008
DRAG_FLOOR = 0.5

BLOCKS = 32
WIDTH = 128
SLOTS = 128
TILES = 36
CELL_DEV = 16
UNROLL = 64
LAG1, LAG2, LAG3 = (3, 4, 5)
TOGETHER = 32
SIDES = (-1, 0, 1)
F32 = jnp.float32
BF16 = jnp.bfloat16
MESH = pl.DeviceIdType.MESH
NT = (((1,), (1,)), ((), ()))
PAIR_SCALE = float(PAIR_STRENGTH * (1.0 / CORE_SQUARED) ** 1.5)
OWN, ON, OFF = 0, 1, 2


def ghost_slot(dx, dy, role):
    return role * 9 + (dx + 1) * 3 + dy + 1


def dot(first, second):
    return jnp.dot(first, second, preferred_element_type=F32)


def dot_nt(first, second):
    return lax.dot_general(first, second, NT, preferred_element_type=F32)


def head(value):
    return value.astype(BF16).astype(F32)


def pair16(low, high):
    return jnp.concatenate([low, high], axis=0).astype(BF16)


def row_ids(shape):
    return lax.broadcasted_iota(jnp.int32, shape, 0)


def block_rows(tile, last, rows):
    turned = pltpu.roll(tile, 5, 0)
    line = jnp.where(rows < 3, turned, tile)
    burgers = jnp.where(rows < 2, pltpu.roll(tile, 2, 0), turned)
    burgers = jnp.where((rows == 2) | (rows == 5), last, burgers)
    return line, burgers


def outer_rows(first, second, rows):
    low = jnp.where(rows < 3, first[0:1], first[1:2]) * second
    low = jnp.where(rows < 6, low, 0.0)
    high = jnp.where(rows < 3, first[2:3] * second, 0.0)
    return low, high


def dist_rows(place, norm_row, one_row, rows):
    return jnp.where(rows < 3, place, jnp.where(rows == 3, norm_row, jnp.where(rows == 4, one_row, 0.0)))


def prepare_block(i, dom, feats, weights_rows):
    rows = row_ids((8, WIDTH))
    tile = dom[i]
    last = dom[32 + (i >> 3), pl.ds(i & 7, 1), :]
    line, burgers = block_rows(tile, last, rows)
    place = jnp.where(rows < 3, tile - 0.5, 0.0)
    norm = jnp.sum(place * place, axis=0, keepdims=True)
    scale = 1.0 / CORE_SQUARED
    same = jnp.concatenate(outer_rows(line, burgers, rows), axis=0)
    same_1 = head(same)
    crossed = jnp.concatenate(outer_rows(burgers, line, rows), axis=0)
    crossed_1 = head(crossed)
    dist = dist_rows(-2.0 * scale * place, scale, scale * norm + 1.0, rows)
    first = head(dist)
    second = head(dist - first)
    third = head(dist - first - second)
    gap = jnp.zeros((16, WIDTH), F32)
    stack = jnp.concatenate([same_1, same_1, same - same_1, gap, first, first, first, second, second, third, gap], axis=0)
    feats[i, 0:WIDTH] = jnp.transpose(stack).astype(BF16)
    stack = jnp.concatenate([crossed_1, crossed_1, crossed - crossed_1, jnp.zeros((80, WIDTH), F32)], axis=0)
    feats[i, WIDTH : 2 * WIDTH] = jnp.transpose(stack).astype(BF16)
    place_first = head(place)
    ones = jnp.where(rows == 3, 1.0, 0.0)
    held = pair16(place_first + ones, place - place_first)
    weights_rows[i] = jnp.concatenate([held, held], axis=1)


def pair_group(group, blocks, codes, dom, ghosts, shifts, feats, weights_rows, own_out, peer_out, unroll):
    rows = row_ids((8, WIDTH))
    centre = jnp.where(rows < 3, 0.5, 0.0)
    def load(u):
        slot = group * unroll + u
        i = blocks[0, slot]
        g = codes[0, slot]
        j = blocks[1, slot]
        tile = ghosts[g, j]
        last = ghosts[g, 32 + (j >> 3), pl.ds(j & 7, 1), :]
        line, burgers = block_rows(tile, last, rows)
        place = jnp.where(rows < 3, tile + shifts[g], 0.0)
        norm = jnp.sum(place * place, axis=0, keepdims=True)
        product = jnp.concatenate(outer_rows(line, burgers, rows), axis=0)
        product_1 = product.astype(BF16)
        product_2 = (product - product_1.astype(F32)).astype(BF16)
        products = jnp.concatenate([product_1, product_2, product_1], axis=0)
        dist = dist_rows(place, norm, 1.0, rows)
        first = head(dist)
        rest = dist - first
        second = head(rest)
        dists = jnp.concatenate(
            [
                jnp.zeros((64, WIDTH), BF16),
                pair16(first, second),
                pair16(rest - second, first),
                pair16(second, first),
                jnp.zeros((16, WIDTH), BF16),
            ],
            axis=0,
        )
        held = pair16(first, second)
        return slot, i, place, products, dists, held

    def multiply(slot, i, place, products, dists, held):
        return dot(feats[i][:, :48], products), dot(feats[i, 0:WIDTH], dists)

    def strength_of(both, dist):
        inv = lax.rsqrt(dist)
        inv_sq = inv * inv
        strength = (inv_sq * inv) * (both[0:128] + both[128:256] * inv_sq)
        high = strength.astype(BF16)
        return high, (strength - high.astype(F32)).astype(BF16)

    def reduce(slot, i, place, products, dists, held, high, low):
        peer = dot(weights_rows[i], jnp.concatenate([high, low], axis=0))
        own = dot_nt(jnp.concatenate([held, held], axis=1), jnp.concatenate([high, low], axis=1))
        peer = peer[0:8] + peer[8:16]
        own = own[0:8] + own[8:16]
        home = dom[i] - centre
        own_out[slot] = home * own[4:5] - own
        peer_out[slot] = place * peer[3:4] - peer

    loaded, outs, strengths = {}, {}, {}
    for turn in range(unroll + LAG1 + LAG2 + LAG3):
        if turn < unroll:
            loaded[turn] = load(turn)
        u = turn - LAG1
        if 0 <= u < unroll:
            outs[u] = multiply(*loaded[u])
        u -= LAG2
        if 0 <= u < unroll:
            strengths[u] = strength_of(*outs.pop(u))
        u -= LAG3
        if 0 <= u < unroll:
            reduce(*loaded.pop(u), *strengths.pop(u))


def slot_table(slot_out, live):
    keep = row_ids((SLOTS, WIDTH)) < live
    parts = [
        jnp.where(keep, PAIR_SCALE * slot_out[:, c, :], 0.0) for c in range(3)
    ]
    table = jnp.concatenate(parts, axis=1)
    first = table.astype(BF16)
    return jnp.concatenate([first, (table - first.astype(F32)).astype(BF16)], axis=0)


def slot_hot(targets, base, count):
    ids = row_ids((count, SLOTS)) + base
    hot = jnp.where(ids == targets, 1.0, 0.0).astype(BF16)
    return jnp.concatenate([hot, hot], axis=1)


def moment_block(b, dom, cells, total):
    rows = row_ids((8, WIDTH))
    tile = dom[b]
    last = dom[32 + (b >> 3), pl.ds(b & 7, 1), :]
    line, burgers = block_rows(tile, last, rows)
    hot = row_ids((CELL_DEV, WIDTH)) == cells[pl.ds(b, 1), :]
    line_1 = head(line)
    line_2 = line - line_1
    burgers = jnp.where(rows < 3, burgers, 0.0)
    burgers_1 = head(burgers)
    burgers_2 = burgers - burgers_1
    zero = jnp.zeros((CELL_DEV, WIDTH), F32)
    spread = [
        jnp.concatenate([jnp.where(hot, part[k : k + 1], zero) for k in range(3)], axis=0).astype(BF16)
        for part in (line_1, line_2)
    ]
    pad = jnp.zeros((8, WIDTH), F32)
    left = jnp.concatenate([pair16(burgers_1, pad), pair16(burgers_1, pad), pair16(burgers_2, pad)], axis=1)
    right = jnp.concatenate([spread[0], spread[1], spread[0]], axis=1)
    return total + dot_nt(left, right)


def node_tables(nodes, node_rows, node_hot):
    def copy_row(b, carry):
        for e in range(2):
            node_rows[e, pl.ds(b, 1), :] = nodes[e : e + 1, pl.ds(pl.multiple_of(b * WIDTH, WIDTH), WIDTH)]
        return carry

    lax.fori_loop(0, BLOCKS, copy_row, 0, unroll=4)
    lanes = lax.broadcasted_iota(jnp.int32, (WIDTH, WIDTH), 1).astype(F32)
    for e in range(2):
        lows = (node_rows[e] & 127).astype(F32)
        turned = jnp.transpose(jnp.concatenate([lows, jnp.zeros((96, WIDTH), F32)], axis=0))
        for b in range(BLOCKS):
            node_hot[b, e * WIDTH : (e + 1) * WIDTH, :] = jnp.where(turned[:, b : b + 1] == lanes, 1.0, 0.0).astype(BF16)


def node_sums(node_rows, node_hot, values, count):
    together = TOGETHER

    def body(turn, total):
        parts, hots = [], []
        for u in range(together):
            b = turn * together + u
            for e in range(2):
                hit = row_ids((32, WIDTH)) == node_rows[e, pl.ds(b, 1), :] >> 7
                rows = [jnp.where(hit, values[c, pl.ds(b, 1), :], 0.0) for c in range(2 * count)]
                parts.append(jnp.concatenate(rows, axis=0).astype(BF16))
            hots.append(node_hot[b])
        return total + dot(jnp.concatenate(parts, axis=1), jnp.concatenate(hots, axis=0))

    return lax.fori_loop(0, BLOCKS // together, body, jnp.zeros((64 * count, WIDTH), F32))


def far_tables():
    index = np.arange(CELL_DEV)
    inner = np.stack([index // 4, index // 2 % 2, index % 2])
    rel = np.arange(256)
    away = np.stack([rel // 64 * 4, (rel // 8 % 8 - 1) * 2, (rel % 8 - 1) * 2])
    delta = away[:, None, None, :] + inner[:, :, None, None] - inner[:, None, :, None]
    delta = (delta + 8) % 16 - 8
    dist = np.sqrt(np.maximum((delta.astype(np.float64) ** 2).sum(0), 1.0))
    far = np.where(np.abs(delta).max(0) > 1, FAR_STRENGTH / dist, 0.0).astype(np.float32)
    lanes = np.arange(384)
    part = lanes % 128
    fold = np.zeros((16, 384), np.float32)
    for lane in lanes[part < 48]:
        fold[3 * (lane // 128) + part[lane] // 16, lane] = 1.0
    return far.reshape(256, 256), fold


def kernel(
    state_in, cells_in, nodes_in, blocks_in, codes_in, count, far_in, fold_in, out,
    raw, cells, nodes, block_ids, code_ids, blocks, codes, far_table, fold,
    dom, ghosts, shifts, feats, weights_rows, own_out, peer_out, react, from_on, from_off, from_layer,
    node_rows, node_hot, node_len, values, group_z, group_xy,
    load_sem, halo_send, halo_recv, react_send, react_recv, gather_send, gather_recv,
):
    size_x, size_y, size_z = 4, 8, 8
    me_x = lax.axis_index("gx")
    me_y = lax.axis_index("gy")
    me_z = lax.axis_index("gz")
    toward = 1 - 2 * lax.rem(me_z, 2)

    loads = [
        pltpu.make_async_copy(source, target, load_sem.at[number])
        for number, (source, target) in enumerate(
            [
                (state_in, raw), (cells_in, cells), (nodes_in, nodes), (blocks_in, blocks), (codes_in, codes),
                (blocks_in, block_ids), (codes_in, code_ids), (far_in, far_table), (fold_in, fold),
            ]
        )
    ]
    for load in loads:
        load.start()

    def at_x(d):
        return lax.rem(me_x + d + size_x, size_x)

    def at_y(d):
        return lax.rem(me_y + d + size_y, size_y)

    def at_z(d):
        return lax.rem(me_z + d + size_z, size_z)

    def away(role):
        return 0 if role == OWN else (toward if role == ON else -toward)

    def device(dx, dy, role):
        return (at_x(dx), at_y(dy), at_z(away(role)))

    def code(dx, dy, dz):
        return (dx + 1) * 9 + (dy + 1) * 3 + dz + 1

    peers = [
        device(-1, 0, OWN), device(1, 0, OWN), device(0, -1, OWN), device(0, 1, OWN), device(0, 0, OFF), device(0, 0, ON)
    ]
    barrier = pltpu.get_barrier_semaphore()
    for peer in peers:
        pl.semaphore_signal(barrier, inc=1, device_id=peer, device_id_type=MESH)
    loads[0].wait()
    for k in range(8):
        dom[0:BLOCKS, k, :] = raw[k]
    dom[BLOCKS:TILES] = raw[8].reshape(4, 8, WIDTH)
    pl.semaphore_wait(barrier, len(peers))

    halo = []
    half = TILES // 2

    def piece(ref, part):
        return ref if part is None else ref.at[pl.ds(part * half, half)]

    def ghost(dx, dy, role):
        return ghosts.at[code(dx, dy, away(role))]

    def send_ghost(source, to, slot, offset, part):
        copy = pltpu.make_async_remote_copy(
            src_ref=piece(source, part),
            dst_ref=piece(ghosts.at[code(*offset)], part),
            send_sem=halo_send.at[len(halo)],
            recv_sem=halo_recv.at[2 * slot + (part or 0)],
            device_id=device(*to),
            device_id_type=MESH,
        )
        copy.start()
        halo.append(copy)

    def await_ghost(dx, dy, role, part=None):
        pltpu.make_async_remote_copy(
            src_ref=piece(dom, part),
            dst_ref=piece(ghost(dx, dy, role), part),
            send_sem=halo_send.at[0],
            recv_sem=halo_recv.at[2 * ghost_slot(dx, dy, role) + (part or 0)],
            device_id=device(0, 0, ON),
            device_id_type=MESH,
        ).wait_recv()

    def pass_x(source, e, dy, role, part):
        send_ghost(source, (e, 0, OWN), ghost_slot(-e, dy, role), (-e, dy, away(role)), part)

    def pass_y(source, e, dx, role, part):
        send_ghost(source, (0, e, OWN), ghost_slot(dx, -e, role), (dx, -e, away(role)), part)

    def pass_off(source, dx, dy, part):
        send_ghost(source, (0, 0, OFF), ghost_slot(dx, dy, OFF), (dx, dy, toward), part)

    def pass_on(source, dx, dy):
        send_ghost(source, (0, 0, ON), ghost_slot(dx, dy, ON), (dx, dy, -toward), None)

    for part in (0, 1):
        for e in (-1, 1):
            pass_y(dom, e, 0, OWN, part)
        for e in (-1, 1):
            pass_x(dom, e, 0, OWN, part)
        pass_off(dom, 0, 0, part)
    pass_on(dom, 0, 0)

    gathers = []

    def gather(source, target, to):
        number = len(gathers)
        copy = pltpu.make_async_remote_copy(
            src_ref=source,
            dst_ref=target,
            send_sem=gather_send.at[number],
            recv_sem=gather_recv.at[number],
            device_id=to,
            device_id_type=MESH,
        )
        copy.start()
        gathers.append(copy)
        return copy

    def spread_of_8(ref_of, at):
        for distance, moves in ((1, ((1, 2, 1, -1), (1, 0, 1, 1))), (3, ((0, 3, 3, -1), (1, 6, 2, 1)))):
            sent = [
                gather(ref_of(first, count), ref_of(target, count), at(sign * distance))
                for first, target, count, sign in moves
            ]
            yield
            for copy in sent:
                copy.wait_recv()

    def gather_steps():
        yield from spread_of_8(
            lambda first, count: group_z.at[pl.ds(8 * first, 8 * count)], lambda d: (me_x, me_y, at_z(d))
        )
        for a in range(3):
            group_xy[0, 1, 8 * a : 8 * a + 8, :] = group_z[pl.ds(a, 8, stride=8), :]
        yield from spread_of_8(
            lambda first, count: group_xy.at[0, pl.ds(first, count)], lambda d: (me_x, at_y(d), me_z)
        )
        sent = [
            gather(group_xy.at[0], group_xy.at[r], (at_x(-r), me_y, me_z)) for r in range(1, size_x)
        ]
        yield
        for copy in sent:
            copy.wait_recv()

    steps = gather_steps()

    def gather_step():
        next(steps, None)

    def features(b, carry):
        prepare_block(b, dom, feats, weights_rows)
        return carry

    def features_part(number):
        lax.fori_loop(4 * number, 4 * number + 4, features, 0, unroll=2)

    loads[1].wait()
    moments = lax.fori_loop(
        0, BLOCKS, lambda b, total: moment_block(b, dom, cells, total), jnp.zeros((16, 48), F32), unroll=4
    )
    group_z[8:16, :] = jnp.concatenate([moments[0:8], jnp.zeros((8, 80), F32)], axis=1)

    for part in (0, 1):
        await_ghost(0, 0, OFF, part)
        for e in (-1, 1):
            pass_x(ghost(0, 0, OFF), e, 0, OFF, part)
    await_ghost(0, 0, ON)
    gather_step()
    features_part(0)
    for part in (0, 1):
        for dx in (-1, 1):
            await_ghost(dx, 0, OWN, part)
            pass_y(ghost(dx, 0, OWN), -dx, dx, OWN, part)
    for dx in (-1, 1):
        pass_on(ghost(dx, 0, OWN), dx, 0)
    features_part(1)
    for part in (0, 1):
        for dy in (-1, 1):
            await_ghost(0, dy, OWN, part)
            pass_x(ghost(0, dy, OWN), dy, dy, OWN, part)
            pass_off(ghost(0, dy, OWN), 0, dy, part)
    for dy in (-1, 1):
        pass_on(ghost(0, dy, OWN), 0, dy)
    gather_step()
    features_part(2)
    for part in (0, 1):
        for dx in (-1, 1):
            await_ghost(dx, 0, OFF, part)
            pass_y(ghost(dx, 0, OFF), dx, dx, OFF, part)
    features_part(3)
    for part in (0, 1):
        for d in (-1, 1):
            await_ghost(d, d, OWN, part)
            pass_off(ghost(d, d, OWN), d, d, part)
    for d in (-1, 1):
        pass_on(ghost(d, d, OWN), d, d)
    gather_step()
    features_part(4)
    for d in (-1, 1):
        for part in (0, 1):
            await_ghost(d, -d, OWN, part)
        pass_on(ghost(d, -d, OWN), d, -d)
    for number in range(5, 8):
        features_part(number)

    ghosts[code(0, 0, 0)] = dom[...]
    rows = row_ids((8, WIDTH))
    for dx in SIDES:
        for dy in SIDES:
            for dz in SIDES:
                shifts[code(dx, dy, dz)] = jnp.where(
                    rows == 0,
                    dx - 0.5,
                    jnp.where(rows == 1, dy - 0.5, jnp.where(rows == 2, dz - 0.5, 0.0)),
                )
    loads[2].wait()
    node_tables(nodes, node_rows, node_hot)
    lines = [raw[3 + k] for k in range(3)]
    length = 0.5 * jnp.sqrt(lines[0] * lines[0] + lines[1] * lines[1] + lines[2] * lines[2])
    values[0] = head(length)
    values[1] = length - head(length)
    sums = node_sums(node_rows, node_hot, values, 1)
    node_len[...] = jnp.maximum(sums[0:32] + sums[32:64], DRAG_FLOOR)
    for load in loads[3:]:
        load.wait()

    for part in (0, 1):
        for dy in (-1, 1):
            await_ghost(0, dy, OFF, part)
        for d in (-1, 1):
            await_ghost(d, -d, OFF, part)
            await_ghost(d, d, OFF, part)
    for dx in SIDES:
        for dy in SIDES:
            if (dx, dy) != (0, 0):
                await_ghost(dx, dy, ON)

    def pair_part(first, last):
        def body(group, carry):
            pair_group(
                group, blocks, codes, dom, ghosts, shifts, feats, weights_rows, own_out, peer_out, UNROLL
            )
            return carry

        lax.fori_loop(first // UNROLL, last // UNROLL, body, 0)

    gather_step()
    pair_part(0, 64)
    gather_step()
    pair_part(64, SLOTS)

    live = count[0]
    table = slot_table(peer_out, live)
    code_row = code_ids[...]
    side = (code_row * 43) >> 7
    away_z = code_row - 3 * side - 1
    role_row = jnp.where(away_z == 0, OWN, jnp.where(away_z == toward, ON, OFF))
    targets = (role_row * 9 + side) * BLOCKS + block_ids[1:2, :]
    reacts = []

    def send_react(source, target_ref, target, number):
        copy = pltpu.make_async_remote_copy(
            src_ref=source,
            dst_ref=target_ref,
            send_sem=react_send.at[number],
            recv_sem=react_recv.at[number],
            device_id=target,
            device_id_type=MESH,
        )
        copy.start()
        reacts.append(copy)

    react[ON] = dot(slot_hot(targets, 288, 288), table)
    send_react(react.at[ON], from_on, device(0, 0, ON), 0)
    react[OFF] = dot(slot_hot(targets, 576, 288), table)
    for dx in SIDES:
        for dy in SIDES:
            d = ghost_slot(dx, dy, 0)
            send_react(
                react.at[OFF, pl.ds(32 * d, 32)], from_off.at[pl.ds(32 * d, 32)], device(dx, dy, OFF), 1 + d
            )
    react[OWN] = dot(slot_hot(targets, 0, 288), table)
    reacts[0].wait_recv()
    react[OWN] = react[OWN] + from_on[...]
    sent = [(dx, dy) for dx in SIDES for dy in SIDES if (dx, dy) != (0, 0)]
    for number, (dx, dy) in enumerate(sent):
        d = ghost_slot(dx, dy, 0)
        send_react(
            react.at[OWN, pl.ds(32 * d, 32)], from_layer.at[number], device(dx, dy, OWN), 10 + number
        )

    near = dot(slot_hot(block_ids[0:1, :], 0, BLOCKS), slot_table(own_out, live))
    near = near + react[OWN, pl.ds(128, 32), :]

    for _ in steps:
        pass
    sides = []
    for a in range(3):
        held = group_xy[:, :, 8 * a : 8 * a + 8, :].reshape(256, WIDTH)
        first = held.astype(BF16)
        second = (held - first.astype(F32)).astype(BF16)
        sides.append(jnp.concatenate([first, second, first], axis=0))
    far = far_table[...]
    first = far.astype(BF16)
    second = (far - first.astype(F32)).astype(BF16)
    spread = dot(jnp.concatenate([first, first, second], axis=1), jnp.concatenate(sides, axis=1))
    source = lax.broadcasted_iota(jnp.int32, (256, 384), 0) >> 4
    lane = lax.broadcasted_iota(jnp.int32, (256, 384), 1) & 15
    spread = jnp.where(source == lane, spread, 0.0)
    folded = spread[0:16]
    for k in range(1, 16):
        folded = folded + spread[16 * k : 16 * k + 16]
    folded = jnp.concatenate([folded, jnp.zeros((112, 384), F32)], axis=0)
    first = folded.astype(BF16)
    second = (folded - first.astype(F32)).astype(BF16)
    folds = fold[...].astype(BF16)
    field = dot_nt(jnp.concatenate([folds, folds], axis=1), jnp.concatenate([first, second], axis=1))
    cell = cells[...]
    hits = [cell == m for m in range(CELL_DEV)]
    per_seg = []
    for m in range(9):
        held = jnp.zeros((BLOCKS, WIDTH), F32)
        for k in range(CELL_DEV):
            held = jnp.where(hits[k], field[m : m + 1, k : k + 1], held)
        per_seg.append(held)
    burgers = [raw[6], raw[7], raw[8]]
    lines = [raw[3 + k] for k in range(3)]
    pulled = [sum(per_seg[3 * a + k] * burgers[k] for k in range(3)) for a in range(3)]
    force = [
        pulled[1] * lines[2] - pulled[2] * lines[1],
        pulled[2] * lines[0] - pulled[0] * lines[2],
        pulled[0] * lines[1] - pulled[1] * lines[0],
    ]

    for d in range(9):
        reacts[1 + d].wait_recv()
        near = near + from_off[pl.ds(32 * d, 32), :]
    for number in range(8):
        reacts[10 + number].wait_recv()
        near = near + from_layer[number]
    for c in range(3):
        half = 0.5 * (force[c] + near[:, 128 * c : 128 * c + 128])
        values[c] = head(half)
        values[3 + c] = half - head(half)
    sums = node_sums(node_rows, node_hot, values, 3)
    for c in range(3):
        out[c] = (sums[32 * c : 32 * c + 32] + sums[96 + 32 * c : 128 + 32 * c]) / node_len[...]

    for copy in halo + gathers + reacts:
        copy.wait_send()


def shards(seg_state, seg_cells, seg_nodes, pair_blocks, pair_offsets, pair_count):
    far_table, fold = far_tables()
    anywhere = pl.BlockSpec(memory_space=pltpu.HBM)
    out = pl.pallas_call(
        kernel,
        out_shape=jax.ShapeDtypeStruct((3, BLOCKS, WIDTH), F32),
        in_specs=[anywhere] * 5 + [pl.BlockSpec(memory_space=pltpu.SMEM)] + [anywhere] * 2,
        out_specs=pl.BlockSpec(memory_space=pltpu.VMEM),
        scratch_shapes=[
            pltpu.VMEM((9, BLOCKS, WIDTH), F32),
            pltpu.VMEM((BLOCKS, WIDTH), jnp.int32),
            pltpu.VMEM((2, BLOCKS * WIDTH), jnp.int32),
            pltpu.VMEM((2, SLOTS), jnp.int32),
            pltpu.VMEM((1, SLOTS), jnp.int32),
            pltpu.SMEM((2, SLOTS), jnp.int32),
            pltpu.SMEM((1, SLOTS), jnp.int32),
            pltpu.VMEM(far_table.shape, F32),
            pltpu.VMEM(fold.shape, F32),
            pltpu.VMEM((TILES, 8, WIDTH), F32),
            pltpu.VMEM((27, TILES, 8, WIDTH), F32),
            pltpu.VMEM((27, 8, WIDTH), F32),
            pltpu.VMEM((BLOCKS, 256, WIDTH), BF16),
            pltpu.VMEM((BLOCKS, 16, 256), BF16),
            pltpu.VMEM((SLOTS, 8, WIDTH), F32),
            pltpu.VMEM((SLOTS, 8, WIDTH), F32),
            pltpu.VMEM((3, 288, 384), F32),
            pltpu.VMEM((288, 384), F32),
            pltpu.VMEM((288, 384), F32),
            pltpu.VMEM((8, 32, 384), F32),
            pltpu.VMEM((2, BLOCKS, WIDTH), jnp.int32),
            pltpu.VMEM((BLOCKS, 256, WIDTH), BF16),
            pltpu.VMEM((32, WIDTH), F32),
            pltpu.VMEM((6, BLOCKS, WIDTH), F32),
            pltpu.VMEM((64, WIDTH), F32),
            pltpu.VMEM((4, 8, 24, WIDTH), F32),
            pltpu.SemaphoreType.DMA((9,)),
            pltpu.SemaphoreType.DMA((43,)),
            pltpu.SemaphoreType.DMA((54,)),
            pltpu.SemaphoreType.DMA((18,)),
            pltpu.SemaphoreType.DMA((18,)),
            pltpu.SemaphoreType.DMA((11,)),
            pltpu.SemaphoreType.DMA((11,)),
        ],
        compiler_params=pltpu.CompilerParams(
            collective_id=0, has_side_effects=True, vmem_limit_bytes=62 * 1024 * 1024
        ),
    )(
        jnp.transpose(seg_state[0, 0, 0], (1, 0, 2)),
        seg_cells[0, 0, 0],
        seg_nodes[0, 0, 0],
        pair_blocks[0, 0, 0],
        pair_offsets[0, 0],
        pair_count.reshape(1),
        jnp.asarray(far_table),
        jnp.asarray(fold),
    )
    return out.reshape(1, 1, 1, 3, BLOCKS * WIDTH)


def solution(mesh):
    placed = (
        P("gx", "gy", "gz", None, None, None),
        P("gx", "gy", "gz", None, None),
        P("gx", "gy", "gz", None, None),
        P("gx", "gy", "gz", None, None),
        P("gx", "gy", "gz", None),
        P("gx", "gy", "gz"),
    )
    return jax.shard_map(
        shards,
        mesh=mesh,
        in_specs=placed,
        out_specs=P("gx", "gy", "gz", None, None),
        check_vma=False,
    )
```
